128 devices in a mesh: gx: 32 (over z_hi, x, y), gy: 4 (over z_lo, core).
Axes of the slice: x: 4, y: 4, z: 4 (z_hi: 2, z_lo: 2; z = z_hi * 2 + z_lo), core: 2. Of those that a mesh axis runs over, the one named last changes fastest.
Arguments:
- populations: float32 [27, 256, 64, 512], P(None, 'gx', 'gy'), as said below
- solid: int32 [256, 64, 512], P('gx', 'gy'), may hold values 0 or 1
- basis: float32 [64, 3, 256, 4096], P(None, None, ('gx', 'gy'))
- singular: float32 [64], replicated, may hold values from 0.5 to 20
- recent: float32 [7, 3, 256, 4096], P(None, None, ('gx', 'gy'))
- age: int32 [8], replicated, may hold values from 0 to 7
Outputs:
- next_populations: float32 [27, 256, 64, 512], P(None, 'gx', 'gy')
- directions: float32 [8, 3, 256, 4096], P(None, None, ('gx', 'gy'))
- core: float32 [72, 72], replicated
The draws below stay inside these ranges and needn't reach their ends.
Inputs may be any that keep to these rules, and one draw needn't show every extreme that they name: `populations`: every population is positive.
All inputs are finite; a program needn't handle non-finite values. No bound on the sum of `solid` on one device may be relied on, other than what follows from the above.
Results may differ from the reference program's by a relative error of at most 0.0003.
Values sent between devices are 32-bit elements; how exact they have to be, the bound alone decides.
A program may use at most 128 MiB of HBM per device.

```python
import math
import jax
import jax.numpy as jnp
from jax import lax

RANK = 64
SNAPS = 8
NX = 256
NY = 64
NZ = 512
NZS = 256
PLANE = 4096


def rising_scale(base_scale, span_ratio):
    ramp = jnp.arange(NZS).astype(jnp.float32) / max(NZS - 1, 1)
    return base_scale * span_ratio ** ramp


def modes_from(key, base_scale, span_ratio):
    normals = jax.random.normal(key, (RANK, 3, NZS, PLANE), jnp.float32)
    return normals * rising_scale(base_scale, span_ratio)[None, None, :, None]


def draw_populations(key, part):
    key = jax.random.fold_in(key, 11)
    key_density, key_speed, key_jitter = jax.random.split(key, 3)
    speed_amp = 0.035
    ripple = 0.2
    grid_shape = (NX, NY, NZ)
    density = jax.random.uniform(key_density, grid_shape, jnp.float32, 0.95, 1.05)
    speeds = jax.random.uniform(key_speed, (3,) + grid_shape, jnp.float32, -speed_amp, speed_amp)
    jitter_part = jax.random.uniform(key_jitter, (27,) + grid_shape, jnp.float32, -ripple, ripple)
    index_all = jnp.arange(27)
    dir_x = (index_all // 9 - 1).astype(jnp.float32)
    dir_y = (index_all // 3 % 3 - 1).astype(jnp.float32)
    dir_z = (index_all % 3 - 1).astype(jnp.float32)
    span_len = jnp.abs(dir_x) + jnp.abs(dir_y) + jnp.abs(dir_z)
    weights = jnp.where(span_len == 0, 8.0 / 27.0, jnp.where(span_len == 1, 2.0 / 27.0, jnp.where(span_len == 2, 1.0 / 54.0, 1.0 / 216.0)))
    along = dir_x[:, None, None, None] * speeds[0] + dir_y[:, None, None, None] * speeds[1] + dir_z[:, None, None, None] * speeds[2]
    speed_sq = speeds[0] * speeds[0] + speeds[1] * speeds[1] + speeds[2] * speeds[2]
    balance = weights[:, None, None, None] * density * (1.0 + 3.0 * along + 4.5 * along * along - 1.5 * speed_sq)
    return (balance * (1.0 + jitter_part)).astype(jnp.float32)


def draw_basis(key, part):
    mode_rows = modes_from(key, 0.6, 3.0)
    return mode_rows


def draw_recent(key, part):
    base_scale = 0.6
    span_ratio = 3.0
    shared = 0.7
    alone = 0.71
    mode_rows = modes_from(key, base_scale, span_ratio)
    key = jax.random.fold_in(key, 5)
    key_coef, key_jitter, key_common = jax.random.split(key, 3)
    coefficients = 0.3 * jax.random.normal(key_coef, (SNAPS - 1, 4), jnp.float32)
    common_part = jax.random.normal(key_common, (1, 3, NZS, PLANE), jnp.float32)
    own_part = jax.random.normal(key_jitter, (SNAPS - 1, 3, NZS, PLANE), jnp.float32)
    jitter_part = 0.5 * (shared * common_part + alone * own_part)
    jitter_part = jitter_part * rising_scale(base_scale, span_ratio)[None, None, :, None]
    column_ids = jnp.arange(SNAPS - 1)
    for term in range(4):
        mode_picks = (4 * column_ids + 17 * term) % RANK
        jitter_part = jitter_part + coefficients[:, term][:, None, None, None] * mode_rows[mode_picks]
    return jitter_part


def place_ends(values, rng, smallest, top_value):
    index_at = [jax.random.randint(jax.random.fold_in(rng, axis), (), 0, length) for axis, length in enumerate(values.shape)]
    widest = values.shape.index(max(values.shape))
    beside = index_at[:widest] + [(index_at[widest] + 1) % values.shape[widest]] + index_at[widest + 1:]
    return values.at[tuple(index_at)].set(smallest).at[tuple(beside)].set(top_value)


def setup_inputs(seed: int = 0) -> dict:
    streams_of = jax.random.split(jax.random.key(seed), 7)
    return {
        "populations": draw_populations(jax.random.fold_in(streams_of[6], 71), 0),
        "solid": place_ends((jax.random.randint(streams_of[1], (NX, NY, NZ), 0, 8) < 1).astype(jnp.int32), jax.random.fold_in(streams_of[1], 1), 0, 1),
        "basis": draw_basis(jax.random.fold_in(streams_of[6], 71), 0),
        "singular": jnp.clip(jnp.exp(jax.random.uniform(streams_of[3], (RANK,), jnp.float32, math.log(0.5), math.log(20.0))), 0.5, 20.0),
        "recent": draw_recent(jax.random.fold_in(streams_of[6], 71), 0),
        "age": place_ends(jax.random.randint(streams_of[5], (SNAPS,), 0, 8), jax.random.fold_in(streams_of[5], 1), 0, 7).astype(jnp.int32),
    }


omega_rate = 1.0 / 0.6
vel_gain = 50.0
age_span = 8.0

def lattice_tables():
    index_all = jnp.arange(27)
    dir_x = (index_all // 9 - 1).astype(jnp.float32)
    dir_y = (index_all // 3 % 3 - 1).astype(jnp.float32)
    dir_z = (index_all % 3 - 1).astype(jnp.float32)
    span_len = jnp.abs(dir_x) + jnp.abs(dir_y) + jnp.abs(dir_z)
    weights = jnp.where(span_len == 0, 8.0 / 27.0, jnp.where(span_len == 1, 2.0 / 27.0, jnp.where(span_len == 2, 1.0 / 54.0, 1.0 / 216.0)))
    return (jnp.stack([dir_x, dir_y, dir_z]), weights.astype(jnp.float32))

def moments(field):
    cubed = field.reshape((3, 3, 3) + field.shape[1:])
    density = jnp.sum(field, axis=0)
    x_speed = (jnp.sum(cubed[2], axis=(0, 1)) - jnp.sum(cubed[0], axis=(0, 1))) / density
    y_speed = (jnp.sum(cubed[:, 2], axis=(0, 1)) - jnp.sum(cubed[:, 0], axis=(0, 1))) / density
    z_speed = (jnp.sum(cubed[:, :, 2], axis=(0, 1)) - jnp.sum(cubed[:, :, 0], axis=(0, 1))) / density
    return (density, x_speed, y_speed, z_speed)

def lower_inverse(factor):
    matrix_order = factor.shape[0]
    unit_rows = jnp.eye(matrix_order, dtype=factor.dtype)
    solved_rows = []
    for row_index in range(matrix_order):
        running = unit_rows[row_index]
        for col_index in range(row_index):
            running = running - factor[row_index, col_index] * solved_rows[col_index]
        solved_rows.append(running / factor[row_index, row_index])
    return jnp.stack(solved_rows)

def reference(populations, solid, basis, singular, recent, age):
    lattice_dirs, weights = lattice_tables()
    density, x_speed, y_speed, z_speed = moments(populations)
    speed_sq = x_speed * x_speed + y_speed * y_speed + z_speed * z_speed
    is_solid = solid > 0
    passed = []
    for i in range(27):
        along = lattice_dirs[0, i] * x_speed + lattice_dirs[1, i] * y_speed + lattice_dirs[2, i] * z_speed
        balance = weights[i] * density * (1.0 + 3.0 * along + 4.5 * along * along - 1.5 * speed_sq)
        relaxed = jnp.where(is_solid, populations[26 - i], populations[i] - omega_rate * (populations[i] - balance))
        offsets = (i // 9 - 1, i // 3 % 3 - 1, i % 3 - 1)
        passed.append(jnp.roll(relaxed, offsets, axis=(0, 1, 2)))
    next_populations = jnp.stack(passed)
    new_density, vx_new, vy_new, vz_new = moments(next_populations)
    sampled = jnp.stack([vx_new, vy_new, vz_new])[:, ::2, ::2, ::2] * vel_gain
    fresh_snap = jnp.transpose(sampled, (0, 3, 1, 2)).reshape(1, 3, sampled.shape[3], sampled.shape[1] * sampled.shape[2])
    snap_block = jnp.concatenate([fresh_snap, recent], 0) * jnp.exp(-age.astype(jnp.float32) / age_span)[:, None, None, None]
    flat_block = snap_block.reshape(snap_block.shape[0], -1)
    mode_rows = basis.reshape(basis.shape[0], -1)
    row_total = float(flat_block.shape[1])
    highest = lax.Precision.HIGHEST
    coefficients = jnp.dot(flat_block, mode_rows.T, precision=highest) / row_total
    residual = flat_block - jnp.dot(coefficients, mode_rows, precision=highest)
    gram_matrix = jnp.dot(residual, residual.T, precision=highest) / row_total
    factor = jnp.linalg.cholesky(gram_matrix)
    inverse_factor = lower_inverse(factor)
    directions = jnp.dot(inverse_factor, residual, precision=highest).reshape(snap_block.shape)
    top_rows = jnp.concatenate([jnp.diag(singular), coefficients.T], 1)
    low_rows = jnp.concatenate([jnp.zeros((factor.shape[0], singular.shape[0]), jnp.float32), factor.T], 1)
    core = jnp.concatenate([top_rows, low_rows], 0)
    return (next_populations, directions, core)
```

```python
import functools

import jax
import jax.numpy as jnp
from jax import lax
from jax.experimental import pallas as pl
from jax.experimental.pallas import tpu as pltpu
from jax.sharding import PartitionSpec as P

MESH = pl.DeviceIdType.MESH
HIGHEST = lax.Precision.HIGHEST
omega_rate = 1.0 / 0.6
keep_rate = 1.0 - omega_rate
vel_gain = 50.0
age_span = 8.0
WEIGHTS = (8.0 / 27.0, 2.0 / 27.0, 1.0 / 54.0, 1.0 / 216.0)
NDEV = 128
RANK = 64
SNAPS = 8
ROWS = 192
TOTAL = 3145728.0


def direction(i):
    return i // 9 - 1, i // 3 % 3 - 1, i % 3 - 1


def shifted(value, shift_y, shift_z):
    if shift_z:
        value = pltpu.roll(value, 1 if shift_z > 0 else value.shape[1] - 1, 1)
    if shift_y:
        value = pltpu.roll(value, 1 if shift_y > 0 else value.shape[0] - 1, 0)
    return value


def collide_plane(x, pops, solid, mo, nxt):
    for piece in range(4):
        lanes = pl.ds(piece * 128, 128)
        total = [None] * 4
        for e in range(3):
            row = [None] * 3
            for f in range(3):
                p0, p1, p2 = (pops[9 * e + 3 * f + g, x, :, lanes] for g in range(3))
                row[f] = (p0 + p1 + p2, p2 - p0)
            dens = row[0][0] + row[1][0] + row[2][0]
            my = row[2][0] - row[0][0]
            mz = row[0][1] + row[1][1] + row[2][1]
            if e == 0:
                total = [dens, -dens, my, mz]
            else:
                total = [
                    total[0] + dens,
                    total[1] + dens if e == 2 else total[1],
                    total[2] + my,
                    total[3] + mz,
                ]
        inv = 1.0 / total[0]
        ux, uy, uz = total[1] * inv, total[2] * inv, total[3] * inv
        scaled = omega_rate * total[0]
        mo[0, :, lanes] = scaled
        mo[1, :, lanes] = ux
        mo[2, :, lanes] = uy
        mo[3, :, lanes] = uz
        mo[4, :, lanes] = scaled * (1.0 - 1.5 * (ux * ux + uy * uy + uz * uz))

    x_up, x_down = lax.rem(x + 1, 8), lax.rem(x + 7, 8)
    place = {0: x, 1: x_up, -1: x_down}
    for pos in range(14, 27):
        neg = 26 - pos
        ex, ey, ez = direction(pos)
        weight = WEIGHTS[abs(ex) + abs(ey) + abs(ez)]
        along = None
        for axis, part in enumerate((ex, ey, ez)):
            if part:
                term = mo[1 + axis]
                if along is None:
                    along = term if part > 0 else -term
                else:
                    along = along + term if part > 0 else along - term
        is_solid = solid[x] > 0
        scaled = mo[0] * along
        even = weight * mo[4] + (4.5 * weight) * (scaled * along)
        odd = (3.0 * weight) * scaled
        p_pos, p_neg = pops[pos, x], pops[neg, x]
        r_pos = jnp.where(is_solid, p_neg, keep_rate * p_pos + (even + odd))
        r_neg = jnp.where(is_solid, p_pos, keep_rate * p_neg + (even - odd))
        nxt[ex + 1, ey + 1, ez + 1, place[ex]] = shifted(r_pos, ey, ez)
        nxt[1 - ex, 1 - ey, 1 - ez, place[-ex]] = shifted(r_neg, -ey, -ez)
    still = pops[13, x]
    nxt[1, 1, 1, x] = jnp.where(solid[x] > 0, still, keep_rate * still + WEIGHTS[0] * mo[4])


def plane_sums(nxt, plane, firsts, lanes):
    inner, outer = None, None
    for e in firsts:
        row = []
        for f in range(3):
            p0, p1, p2 = (nxt[e, f, g, plane, :, lanes] for g in range(3))
            row.append((p0 + p1 + p2, p2 - p0))
        dens = row[0][0] + row[1][0]
        now_in = [dens, (e - 1) * dens if e != 1 else None, -row[0][0], row[0][1] + row[1][1]]
        now_out = [row[2][0], (e - 1) * row[2][0] if e != 1 else None, row[2][0], row[2][1]]
        if inner is None:
            inner, outer = now_in, now_out
        else:
            inner = [a if b is None else b if a is None else a + b for a, b in zip(inner, now_in)]
            outer = [a if b is None else b if a is None else a + b for a, b in zip(outer, now_out)]
    return inner, outer


def main_kernel(
    pops_in, solid_in, modes_in, recent_in, age_in,
    nxt, resid, small,
    pops, solid, modes, snaps, mo, sums, mxw, mxs, mxr, mys, myr, mcs, mcr,
    field, turned, parcel, arrived, xr_up, xr_dn, yr_up, yr_dn, corner,
    stack, mine1, got1, mine2, got2, mine3, got3, spread,
    load_sem, small_ssem, small_rsem, bulk_ssem, bulk_rsem, ex_ssem, ex_rsem, fix_sem,
):
    gx, gy = lax.axis_index("gx"), lax.axis_index("gy")
    me = gx * 4 + gy
    gx_up, gx_dn = lax.rem(gx + 1, 32), lax.rem(gx + 31, 32)
    gy_up, gy_dn = lax.rem(gy + 1, 4), lax.rem(gy + 3, 4)

    solid_copy = pltpu.make_async_copy(solid_in, solid, load_sem.at[8])
    solid_copy.start()

    def plane_copy(x):
        return pltpu.make_async_copy(pops_in.at[:, x], pops.at[:, x], load_sem.at[x])

    for x in (7, 0, 1, 2, 3, 4, 5, 6):
        plane_copy(x).start()
    recent_copy = pltpu.make_async_copy(recent_in, snaps.at[pl.ds(ROWS, 7 * ROWS)], load_sem.at[9])
    recent_copy.start()
    modes_copy = pltpu.make_async_copy(modes_in, modes, load_sem.at[10])
    modes_copy.start()

    z_hi, x_at, y_at = lax.div(gx, 16), lax.rem(lax.div(gx, 4), 4), lax.rem(gx, 4)
    z_lo, core_at = lax.div(gy, 2), lax.rem(gy, 2)
    z_part = [lax.rem(z_hi + 1 + j, 2) * 16 for j in range(2)]
    x_part = [lax.rem(x_at + 2 + j, 4) * 4 for j in range(4)]
    y_part = [lax.rem(y_at + 2 + j, 4) for j in range(4)]
    lo_part = [lax.rem(z_lo + j, 2) * 2 for j in range(2)]
    core_part = [lax.rem(core_at + j, 2) for j in range(2)]
    peers = []
    for jx in (0, 1, 3, 2):
        for jy in (0, 1, 3, 2):
            for jz in range(2):
                for jl in range(2):
                    for jc in range(2):
                        if (jx, jy, jz, jl, jc) != (2, 2, 1, 0, 0):
                            peers.append((z_part[jz] + x_part[jx] + y_part[jy], lo_part[jl] + core_part[jc]))

    barrier = pltpu.get_barrier_semaphore()
    for peer in peers:
        pl.semaphore_signal(barrier, inc=1, device_id=peer, device_id_type=MESH)

    solid_copy.wait()

    def collide(k, carry):
        x = lax.rem(k + 7, 8)
        plane_copy(x).wait()
        collide_plane(x, pops, solid, mo, nxt)
        return carry

    lax.fori_loop(0, 8, collide, 0)

    row_id = lax.broadcasted_iota(jnp.int32, (16, 128), 0)
    for piece in range(4):
        lanes = pl.ds(piece * 128, 128)
        inner, outer = plane_sums(nxt, 0, (2,), lanes)
        for slot, q in enumerate((0, 2, 3)):
            mxw[slot * 4 + piece] = inner[q] + jnp.where(row_id > 0, outer[q], 0.0)
            mxs[slot * 4 + piece] = mxw[slot * 4 + piece, pl.ds(0, 8, stride=2), :]
        mcs[piece, 0:1, :] = outer[0][0:1]
        mcs[piece, 1:2, :] = outer[3][0:1]
        for n, plane in enumerate((0, 2, 4, 6)):
            inner, outer = plane_sums(nxt, plane, (0, 1) if plane == 0 else (0, 1, 2), lanes)
            for q in range(4):
                sums[(n * 4 + q) * 4 + piece] = inner[q] + jnp.where(row_id > 0, outer[q], 0.0)
            for slot, q in enumerate((0, 1, 3)):
                r = n * 3 + slot
                mys[piece, r : r + 1, :] = outer[q][0:1]

    pl.semaphore_wait(barrier, NDEV - 1)

    def remote(src, dst, ssem, rsem, to):
        return pltpu.make_async_remote_copy(
            src_ref=src, dst_ref=dst, send_sem=ssem, recv_sem=rsem, device_id=to, device_id_type=MESH
        )

    heralds = [
        remote(mxs, mxr, small_ssem.at[0], small_rsem.at[0], (gx_up, gy)),
        remote(mcs, mcr, small_ssem.at[1], small_rsem.at[1], (gx_up, gy_up)),
        remote(mys, myr, small_ssem.at[2], small_rsem.at[2], (gx, gy_up)),
    ]
    for copy in heralds:
        copy.start()
    for copy in heralds:
        copy.wait_recv()

    first_row = lax.broadcasted_iota(jnp.int32, (8, 128), 0) == 0
    for piece in range(4):
        for n in range(4):
            dens, mx, my, mz = (
                sums[(n * 4 + q) * 4 + piece, pl.ds(0, 8, stride=2), :] for q in range(4)
            )
            rows = [jnp.where(first_row, myr[piece, n * 3 + s : n * 3 + s + 1, :], 0.0) for s in range(3)]
            dens, mx, my, mz = dens + rows[0], mx + rows[1], my + rows[0], mz + rows[2]
            if n == 0:
                part = [mxr[s * 4 + piece] for s in range(3)]
                edge = [jnp.where(first_row, mcr[piece, s : s + 1, :], 0.0) for s in range(2)]
                both = part[0] + edge[0]
                dens, mx, my, mz = dens + both, mx + both, my + part[1] + edge[0], mz + part[2] + edge[1]
            scale = vel_gain / dens
            field[piece, n * 32 : n * 32 + 8, :] = mx * scale
            field[piece, n * 32 + 8 : n * 32 + 16, :] = my * scale
            field[piece, n * 32 + 16 : n * 32 + 24, :] = mz * scale
            field[piece, n * 32 + 24 : n * 32 + 32, :] = jnp.zeros((8, 128), jnp.float32)
        turned[piece * 128 : (piece + 1) * 128, :] = jnp.transpose(field[piece])
    for b in range(2):
        parcel[pl.ds(b, NDEV, stride=2), :] = turned[pl.ds(2 * b, NDEV, stride=4), :]

    def to_all(source, target, index, rows):
        place = target.at[pl.ds(me * rows, rows)]
        for peer in peers:
            remote(source(peer), place, ex_ssem.at[index], ex_rsem.at[index], peer).start()
        pltpu.make_async_copy(source((gx, gy)), place, ex_rsem.at[index]).start()

    def all_here(target, index):
        pltpu.make_async_copy(target, target, ex_rsem.at[index]).wait()

    def all_sent(target, index, rows):
        part = target.at[pl.ds(0, (NDEV - 1) * rows)]
        pltpu.make_async_copy(part, part, ex_ssem.at[index]).wait()

    to_all(lambda peer: parcel.at[pl.ds(2 * (peer[0] * 4 + peer[1]), 2)], arrived, 0, 2)

    faces = [
        remote(nxt.at[2, :, :, 0], xr_up, bulk_ssem.at[0], bulk_rsem.at[0], (gx_up, gy)),
        remote(nxt.at[0, :, :, 7], xr_dn, bulk_ssem.at[1], bulk_rsem.at[1], (gx_dn, gy)),
        remote(nxt.at[:, 2, :, :, pl.ds(0, 1)], yr_up, bulk_ssem.at[2], bulk_rsem.at[2], (gx, gy_up)),
        remote(nxt.at[:, 0, :, :, pl.ds(15, 1)], yr_dn, bulk_ssem.at[3], bulk_rsem.at[3], (gx, gy_dn)),
        remote(nxt.at[2, 2, :, 0, pl.ds(0, 1)], corner.at[0], bulk_ssem.at[4], bulk_rsem.at[4], (gx_up, gy_up)),
        remote(nxt.at[2, 0, :, 0, pl.ds(15, 1)], corner.at[1], bulk_ssem.at[5], bulk_rsem.at[5], (gx_up, gy_dn)),
        remote(nxt.at[0, 2, :, 7, pl.ds(0, 1)], corner.at[2], bulk_ssem.at[6], bulk_rsem.at[6], (gx_dn, gy_up)),
        remote(nxt.at[0, 0, :, 7, pl.ds(15, 1)], corner.at[3], bulk_ssem.at[7], bulk_rsem.at[7], (gx_dn, gy_dn)),
    ]
    for copy in faces:
        copy.start()

    decay = [
        jnp.exp(jnp.full((8, 128), age_in[j], jnp.int32).astype(jnp.float32) * (-1.0 / age_span))
        for j in range(SNAPS)
    ]
    recent_copy.wait()
    for j in range(1, SNAPS):
        for k in range(24):
            at = pl.ds(j * ROWS + k * 8, 8)
            snaps[at, :] = snaps[at, :] * decay[j]
    modes_copy.wait()

    def project(block, carry):
        base = block * (4 * ROWS)
        acc = [[None] * 4 for _ in range(7)]
        for k in range(24):
            u = [modes[pl.ds(pl.multiple_of(base + n * ROWS + k * 8, 8), 8), :] for n in range(4)]
            for j in range(7):
                a = snaps[pl.ds((j + 1) * ROWS + k * 8, 8), :]
                for n in range(4):
                    term = a * u[n]
                    acc[j][n] = term if acc[j][n] is None else acc[j][n] + term
        for j in range(7):
            rows = [jnp.sum(acc[j][n], axis=0, keepdims=True) for n in range(4)]
            for n in range(4):
                stack[pl.ds((j + 1) * RANK + block * 4 + n, 1), :] = rows[n]
        return carry

    lax.fori_loop(0, RANK // 4, project, 0)
    ones = jnp.ones((8, 128), jnp.float32)

    def row_totals(block):
        return lax.dot_general(
            ones, block, (((1,), (1,)), ((), ())), precision=HIGHEST, preferred_element_type=jnp.float32
        )

    mine1[...] = jnp.zeros((8, 128), jnp.float32)
    for j in range(1, SNAPS):
        mine1[j : j + 1, 0:RANK] = row_totals(stack[j * RANK : (j + 1) * RANK, :])[0:1]
    to_all(lambda peer: mine1, got1, 1, 8)

    all_here(arrived, 0)
    lane = lax.broadcasted_iota(jnp.int32, (32, 128), 1)
    lane_block = lax.rem(lax.div(lane, 8), 4)
    for b in range(2):
        pieces = [arrived[pl.ds(2 * g + b, 32, stride=8), :] for g in range(4)]
        for c in range(3):
            out = None
            for g in range(4):
                moved = pieces[g] if g == c else pltpu.roll(pieces[g], ((g - c) * 8) % 128, 1)
                out = moved if out is None else jnp.where(lane_block == g, moved, out)
            snaps[pl.ds(c * 64 + b, 32, stride=2), :] = out
    fresh = [snaps[k * 8 : (k + 1) * 8, :] * decay[0] for k in range(24)]
    for k in range(24):
        snaps[k * 8 : (k + 1) * 8, :] = fresh[k]

    def project_fresh(block, carry):
        base = block * (8 * ROWS)
        for n in range(8):
            acc = None
            for k in range(24):
                at = pl.ds(pl.multiple_of(base + n * ROWS + k * 8, 8), 8)
                term = snaps[k * 8 : (k + 1) * 8, :] * modes[at, :]
                acc = term if acc is None else acc + term
            stack[pl.ds(block * 8 + n, 1), :] = jnp.sum(acc, axis=0, keepdims=True)
        return carry

    lax.fori_loop(0, RANK // 8, project_fresh, 0)
    mine2[...] = jnp.zeros((8, 128), jnp.float32)
    mine2[0:1, 0:RANK] = row_totals(stack[0:RANK, :])[0:1]
    to_all(lambda peer: mine2.at[pl.ds(0, 1)], got2, 2, 1)

    for copy in heralds:
        copy.wait_send()
    for copy in faces:
        copy.wait()
    fixes = [
        [
            pltpu.make_async_copy(xr_up, nxt.at[2, :, :, 0], fix_sem.at[0]),
            pltpu.make_async_copy(xr_dn, nxt.at[0, :, :, 7], fix_sem.at[1]),
        ],
        [
            pltpu.make_async_copy(yr_up, nxt.at[:, 2, :, :, pl.ds(0, 1)], fix_sem.at[2]),
            pltpu.make_async_copy(yr_dn, nxt.at[:, 0, :, :, pl.ds(15, 1)], fix_sem.at[3]),
        ],
        [
            pltpu.make_async_copy(corner.at[0], nxt.at[2, 2, :, 0, pl.ds(0, 1)], fix_sem.at[4]),
            pltpu.make_async_copy(corner.at[1], nxt.at[2, 0, :, 0, pl.ds(15, 1)], fix_sem.at[5]),
            pltpu.make_async_copy(corner.at[2], nxt.at[0, 2, :, 7, pl.ds(0, 1)], fix_sem.at[6]),
            pltpu.make_async_copy(corner.at[3], nxt.at[0, 0, :, 7, pl.ds(15, 1)], fix_sem.at[7]),
        ],
    ]
    for copy in fixes[0]:
        copy.start()

    all_here(got1, 1)
    total = got1[0:8, :]
    for d in range(1, NDEV):
        total = total + got1[d * 8 : (d + 1) * 8, :]
    total = total * (1.0 / TOTAL)
    small[0:8, :] = total

    def spread_row(j, row):
        spread[j * 128 : (j + 1) * 128, :] = jnp.transpose(jnp.broadcast_to(row, (128, 128)))

    for j in range(1, SNAPS):
        spread_row(j, total[j : j + 1])

    def subtract(k, carry):
        base = k * 32
        acc = [
            [snaps[pl.ds(pl.multiple_of(base + j * ROWS + n * 8, 8), 8), :] for n in range(4)]
            for j in range(1, SNAPS)
        ]

        for m in range(RANK):
            u = [modes[pl.ds(pl.multiple_of(base + m * ROWS + n * 8, 8), 8), :] for n in range(4)]
            for j in range(7):
                c = spread[(j + 1) * 128 + m : (j + 1) * 128 + m + 1, :]
                for n in range(4):
                    acc[j][n] = acc[j][n] - c * u[n]
        for j in range(7):
            for n in range(4):
                resid[pl.ds(pl.multiple_of(base + (j + 1) * ROWS + n * 8, 8), 8), :] = acc[j][n]
        return carry

    lax.fori_loop(0, ROWS // 32, subtract, 0)

    def inner_product(i, j):
        acc = None
        for k in range(24):
            term = resid[i * ROWS + k * 8 : i * ROWS + k * 8 + 8, :] * resid[j * ROWS + k * 8 : j * ROWS + k * 8 + 8, :]
            acc = term if acc is None else acc + term
        return jnp.sum(acc, axis=0, keepdims=True)

    stack[0 : 2 * RANK, :] = jnp.zeros((2 * RANK, 128), jnp.float32)
    for i in range(1, SNAPS):
        for j in range(1, i + 1):
            stack[i * 8 + j : i * 8 + j + 1, :] = inner_product(i, j)

    for copy in fixes[0]:
        copy.wait()
    for copy in fixes[1]:
        copy.start()
    for copy in fixes[1]:
        copy.wait()
    for copy in fixes[2]:
        copy.start()

    all_here(got2, 2)
    row = jnp.sum(got2[...], axis=0, keepdims=True) * (1.0 / TOTAL)
    small[0:1, :] = row
    spread_row(0, row)

    def subtract_fresh(k, carry):
        base = k * 64
        acc = [snaps[pl.ds(pl.multiple_of(base + n * 8, 8), 8), :] for n in range(8)]
        for m in range(RANK):
            c = spread[m : m + 1, :]
            for n in range(8):
                acc[n] = acc[n] - c * modes[pl.ds(pl.multiple_of(base + m * ROWS + n * 8, 8), 8), :]
        for n in range(8):
            resid[pl.ds(pl.multiple_of(base + n * 8, 8), 8), :] = acc[n]
        return carry

    lax.fori_loop(0, ROWS // 64, subtract_fresh, 0)
    for i in range(SNAPS):
        stack[i * 8 : i * 8 + 1, :] = inner_product(i, 0)
    mine3[...] = jnp.zeros((8, 128), jnp.float32)
    mine3[0:1, :] = row_totals(stack[0:128, :])[0:1]
    to_all(lambda peer: mine3.at[pl.ds(0, 1)], got3, 3, 1)
    for copy in fixes[2]:
        copy.wait()
    all_sent(arrived, 0, 2)
    all_sent(got1, 1, 8)
    all_sent(got2, 2, 1)
    all_here(got3, 3)
    small[8:16, :] = jnp.broadcast_to(jnp.sum(got3[...], axis=0, keepdims=True) * (1.0 / TOTAL), (8, 128))
    all_sent(got3, 3, 1)


def last_kernel(nxt, resid, small, singular, nxt_out, dirs_out, core_out, dirs, gram, wide, sem):
    bulk = pltpu.make_async_copy(nxt, nxt_out, sem.at[0])
    bulk.start()
    gram[...] = jnp.transpose(jnp.broadcast_to(small[8:9, :], (128, 128)))
    low = [[None] * SNAPS for _ in range(SNAPS)]
    inv_diag = [None] * SNAPS
    for j in range(SNAPS):
        diag = gram[j * 8 + j : j * 8 + j + 1, :]
        for k in range(j):
            diag = diag - low[j][k] * low[j][k]
        low[j][j] = jnp.sqrt(diag)
        inv_diag[j] = 1.0 / low[j][j]
        for i in range(j + 1, SNAPS):
            value = gram[i * 8 + j : i * 8 + j + 1, :]
            for k in range(j):
                value = value - low[i][k] * low[j][k]
            low[i][j] = value * inv_diag[j]
    inverse = [[None] * SNAPS for _ in range(SNAPS)]
    for j in range(SNAPS):
        inverse[j][j] = inv_diag[j]
        for i in range(j + 1, SNAPS):
            value = None
            for k in range(j, i):
                term = low[i][k] * inverse[k][j]
                value = term if value is None else value + term
            inverse[i][j] = -value * inv_diag[i]
    for i in range(SNAPS):
        factors = [jnp.broadcast_to(inverse[i][j], (8, 128)) for j in range(i + 1)]
        for k in range(24):
            acc = None
            for j in range(i + 1):
                term = factors[j] * resid[j * ROWS + k * 8 : j * ROWS + k * 8 + 8, :]
                acc = term if acc is None else acc + term
            dirs[i * ROWS + k * 8 : i * ROWS + k * 8 + 8, :] = acc
    out = pltpu.make_async_copy(dirs, dirs_out, sem.at[1])
    out.start()

    row_id = lax.broadcasted_iota(jnp.int32, (RANK, 128), 0)
    lane_id = lax.broadcasted_iota(jnp.int32, (RANK, 128), 1)
    wide[...] = jnp.zeros((128, 128), jnp.float32)
    wide[127:128, 0:RANK] = singular[...]
    wide[0:RANK, :] = jnp.where(row_id == lane_id, jnp.broadcast_to(wide[127:128, :], (RANK, 128)), 0.0)
    row8 = lax.broadcasted_iota(jnp.int32, (8, 128), 0)
    lane8 = lax.broadcasted_iota(jnp.int32, (8, 128), 1)
    block = jnp.where(lane8 < RANK, small[0:8, :], 0.0)
    for i in range(SNAPS):
        for j in range(i + 1):
            block = jnp.where((row8 == i) & (lane8 == RANK + j), low[i][j], block)
    wide[RANK : RANK + 8, :] = block
    core_out[...] = jnp.transpose(wide[...])[0 : RANK + 8, 0 : RANK + 8]
    bulk.wait()
    out.wait()


def per_device(populations, solid, basis, singular, recent, age):
    f32 = jnp.float32
    vmem, hbm, smem = pltpu.VMEM, pltpu.HBM, pltpu.SMEM
    modes = basis.reshape(RANK, 3, 2, 32, 128).transpose(0, 1, 3, 2, 4).reshape(RANK * ROWS, 128)
    earlier = recent.reshape(7, 3, 2, 32, 128).transpose(0, 1, 3, 2, 4).reshape(7 * ROWS, 128)
    dma = pltpu.SemaphoreType.DMA
    in_hbm = pl.BlockSpec(memory_space=hbm)
    in_vmem = pl.BlockSpec(memory_space=vmem)
    nxt, resid, small = pl.pallas_call(
        main_kernel,
        out_shape=(
            vmem((3, 3, 3, 8, 16, 512), f32),
            vmem((SNAPS * ROWS, 128), f32),
            vmem((16, 128), f32),
        ),
        in_specs=[in_hbm, in_hbm, in_hbm, in_hbm, pl.BlockSpec(memory_space=smem)],
        out_specs=(in_vmem, in_vmem, in_vmem),
        scratch_shapes=[
            vmem((27, 8, 16, 512), f32),
            vmem((8, 16, 512), jnp.int32),
            vmem((RANK * ROWS, 128), f32),
            vmem((SNAPS * ROWS, 128), f32),
            vmem((5, 16, 512), f32),
            vmem((64, 16, 128), f32),
            vmem((12, 16, 128), f32),
            vmem((12, 8, 128), f32),
            vmem((12, 8, 128), f32),
            vmem((4, 16, 128), f32),
            vmem((4, 16, 128), f32),
            vmem((4, 8, 128), f32),
            vmem((4, 8, 128), f32),
            vmem((4, 128, 128), f32),
            vmem((512, 128), f32),
            vmem((2 * NDEV, 128), f32),
            vmem((2 * NDEV, 128), f32),
            vmem((3, 3, 16, 512), f32),
            vmem((3, 3, 16, 512), f32),
            vmem((3, 3, 8, 1, 512), f32),
            vmem((3, 3, 8, 1, 512), f32),
            vmem((4, 3, 1, 512), f32),
            vmem((SNAPS * RANK, 128), f32),
            vmem((8, 128), f32),
            vmem((NDEV * 8, 128), f32),
            vmem((8, 128), f32),
            vmem((NDEV, 128), f32),
            vmem((8, 128), f32),
            vmem((NDEV, 128), f32),
            vmem((SNAPS * 128, 128), f32),
            dma((11,)),
            dma((3,)),
            dma((3,)),
            dma((8,)),
            dma((8,)),
            dma((4,)),
            dma((4,)),
            dma((8,)),
        ],
        compiler_params=pltpu.CompilerParams(
            collective_id=0, has_side_effects=True, vmem_limit_bytes=40 * 2**20
        ),
    )(populations, solid, modes, earlier, age)
    nxt_out, dirs, core = pl.pallas_call(
        last_kernel,
        out_shape=(
            jax.ShapeDtypeStruct((3, 3, 3, 8, 16, 512), f32),
            jax.ShapeDtypeStruct((SNAPS * ROWS, 128), f32),
            jax.ShapeDtypeStruct((RANK + 8, RANK + 8), f32),
        ),
        in_specs=[in_vmem, in_vmem, in_vmem, in_vmem],
        out_specs=(in_hbm, in_hbm, in_vmem),
        scratch_shapes=[vmem((SNAPS * ROWS, 128), f32), vmem((128, 128), f32), vmem((128, 128), f32), dma((2,))],
        compiler_params=pltpu.CompilerParams(vmem_limit_bytes=24 * 2**20),
    )(nxt, resid, small, singular.reshape(1, RANK))
    directions = dirs.reshape(SNAPS, 3, 32, 2, 128).transpose(0, 1, 3, 2, 4).reshape(SNAPS, 3, 2, 4096)
    return nxt_out.reshape(27, 8, 16, 512), directions, core


def solution(mesh):
    return jax.shard_map(
        per_device,
        mesh=mesh,
        in_specs=(
            P(None, "gx", "gy", None),
            P("gx", "gy", None),
            P(None, None, ("gx", "gy"), None),
            P(),
            P(None, None, ("gx", "gy"), None),
            P(),
        ),
        out_specs=(P(None, "gx", "gy", None), P(None, None, ("gx", "gy"), None), P()),
        check_vma=False,
    )
```

```python
import functools

import jax
import jax.numpy as jnp
from jax import lax
from jax.experimental import pallas as pl
from jax.experimental.pallas import tpu as pltpu
from jax.sharding import PartitionSpec as P

MESH = pl.DeviceIdType.MESH
HIGHEST = lax.Precision.HIGHEST
omega_rate = 1.0 / 0.6
keep_rate = 1.0 - omega_rate
vel_gain = 50.0
age_span = 8.0
WEIGHTS = (8.0 / 27.0, 2.0 / 27.0, 1.0 / 54.0, 1.0 / 216.0)
NDEV = 128
RANK = 64
SNAPS = 8
ROWS = 192
TOTAL = 3145728.0


def direction(i):
    return i // 9 - 1, i // 3 % 3 - 1, i % 3 - 1


def shifted(value, shift_y, shift_z):
    if shift_z:
        value = pltpu.roll(value, 1 if shift_z > 0 else value.shape[1] - 1, 1)
    if shift_y:
        value = pltpu.roll(value, 1 if shift_y > 0 else value.shape[0] - 1, 0)
    return value


def collide_plane(x, pops, solid, mo, nxt):
    for piece in range(4):
        lanes = pl.ds(piece * 128, 128)
        total = [None] * 4
        for e in range(3):
            row = [None] * 3
            for f in range(3):
                p0, p1, p2 = (pops[9 * e + 3 * f + g, x, :, lanes] for g in range(3))
                row[f] = (p0 + p1 + p2, p2 - p0)
            dens = row[0][0] + row[1][0] + row[2][0]
            my = row[2][0] - row[0][0]
            mz = row[0][1] + row[1][1] + row[2][1]
            if e == 0:
                total = [dens, -dens, my, mz]
            else:
                total = [
                    total[0] + dens,
                    total[1] + dens if e == 2 else total[1],
                    total[2] + my,
                    total[3] + mz,
                ]
        inv = 1.0 / total[0]
        ux, uy, uz = total[1] * inv, total[2] * inv, total[3] * inv
        scaled = omega_rate * total[0]
        mo[0, :, lanes] = scaled
        mo[1, :, lanes] = ux
        mo[2, :, lanes] = uy
        mo[3, :, lanes] = uz
        mo[4, :, lanes] = scaled * (1.0 - 1.5 * (ux * ux + uy * uy + uz * uz))

    x_up, x_down = lax.rem(x + 1, 8), lax.rem(x + 7, 8)
    place = {0: x, 1: x_up, -1: x_down}
    for pos in range(14, 27):
        neg = 26 - pos
        ex, ey, ez = direction(pos)
        weight = WEIGHTS[abs(ex) + abs(ey) + abs(ez)]
        along = None
        for axis, part in enumerate((ex, ey, ez)):
            if part:
                term = mo[1 + axis]
                if along is None:
                    along = term if part > 0 else -term
                else:
                    along = along + term if part > 0 else along - term
        is_solid = solid[x] > 0
        scaled = mo[0] * along
        even = weight * mo[4] + (4.5 * weight) * (scaled * along)
        odd = (3.0 * weight) * scaled
        p_pos, p_neg = pops[pos, x], pops[neg, x]
        r_pos = jnp.where(is_solid, p_neg, keep_rate * p_pos + (even + odd))
        r_neg = jnp.where(is_solid, p_pos, keep_rate * p_neg + (even - odd))
        nxt[ex + 1, ey + 1, ez + 1, place[ex]] = shifted(r_pos, ey, ez)
        nxt[1 - ex, 1 - ey, 1 - ez, place[-ex]] = shifted(r_neg, -ey, -ez)
    still = pops[13, x]
    nxt[1, 1, 1, x] = jnp.where(solid[x] > 0, still, keep_rate * still + WEIGHTS[0] * mo[4])


def plane_sums(nxt, plane, firsts, lanes):
    inner, outer = None, None
    for e in firsts:
        row = []
        for f in range(3):
            p0, p1, p2 = (nxt[e, f, g, plane, :, lanes] for g in range(3))
            row.append((p0 + p1 + p2, p2 - p0))
        dens = row[0][0] + row[1][0]
        now_in = [dens, (e - 1) * dens if e != 1 else None, -row[0][0], row[0][1] + row[1][1]]
        now_out = [row[2][0], (e - 1) * row[2][0] if e != 1 else None, row[2][0], row[2][1]]
        if inner is None:
            inner, outer = now_in, now_out
        else:
            inner = [a if b is None else b if a is None else a + b for a, b in zip(inner, now_in)]
            outer = [a if b is None else b if a is None else a + b for a, b in zip(outer, now_out)]
    return inner, outer


def main_kernel(
    pops_in, solid_in, modes_in, recent_in, age_in,
    nxt, resid, small,
    pops, solid, modes, snaps, mo, sums, field, beyond, turned, parcel, arrived, xr_up, xr_dn, yr_up, yr_dn, corner,
    stack, mine1, got1, mine2, got2, mine3, got3, spread,
    age, load_sem, bulk_ssem, bulk_rsem, ex_ssem, ex_rsem, fix_sem,
):
    gx, gy = lax.axis_index("gx"), lax.axis_index("gy")
    me = gx * 4 + gy
    gx_up, gx_dn = lax.rem(gx + 1, 32), lax.rem(gx + 31, 32)
    gy_up, gy_dn = lax.rem(gy + 1, 4), lax.rem(gy + 3, 4)

    solid_copy = pltpu.make_async_copy(solid_in, solid, load_sem.at[8])
    solid_copy.start()

    def plane_copy(x):
        return pltpu.make_async_copy(pops_in.at[:, x], pops.at[:, x], load_sem.at[x])

    for x in (7, 0, 1, 2, 3, 4, 5, 6):
        plane_copy(x).start()
    recent_copy = pltpu.make_async_copy(recent_in, snaps.at[pl.ds(ROWS, 7 * ROWS)], load_sem.at[9])
    recent_copy.start()
    modes_copy = pltpu.make_async_copy(modes_in, modes, load_sem.at[10])
    modes_copy.start()
    age_copy = pltpu.make_async_copy(age_in, age, load_sem.at[11])
    age_copy.start()

    z_hi, x_at, y_at = lax.div(gx, 16), lax.rem(lax.div(gx, 4), 4), lax.rem(gx, 4)
    z_lo, core_at = lax.div(gy, 2), lax.rem(gy, 2)
    z_part = [lax.rem(z_hi + 1 + j, 2) * 16 for j in range(2)]
    x_part = [lax.rem(x_at + 2 + j, 4) * 4 for j in range(4)]
    y_part = [lax.rem(y_at + 2 + j, 4) for j in range(4)]
    lo_part = [lax.rem(z_lo + j, 2) * 2 for j in range(2)]
    core_part = [lax.rem(core_at + j, 2) for j in range(2)]
    peers = []
    for jx in (0, 1, 3, 2):
        for jy in (0, 1, 3, 2):
            for jz in range(2):
                for jl in range(2):
                    for jc in range(2):
                        if (jx, jy, jz, jl, jc) != (2, 2, 1, 0, 0):
                            peers.append((z_part[jz] + x_part[jx] + y_part[jy], lo_part[jl] + core_part[jc]))

    barrier = pltpu.get_barrier_semaphore()
    for peer in peers:
        pl.semaphore_signal(barrier, inc=1, device_id=peer, device_id_type=MESH)

    solid_copy.wait()

    def collide(k, carry):
        x = lax.rem(k + 7, 8)
        plane_copy(x).wait()
        collide_plane(x, pops, solid, mo, nxt)
        return carry

    lax.fori_loop(0, 8, collide, 0)

    row_id = lax.broadcasted_iota(jnp.int32, (16, 128), 0)
    first_row = lax.broadcasted_iota(jnp.int32, (8, 128), 0) == 0
    second_row = lax.broadcasted_iota(jnp.int32, (8, 128), 0) == 1

    def edge_rows(outer):
        return [jnp.broadcast_to(value[0:1], (8, 128)) for value in outer]

    for piece in range(4):
        lanes = pl.ds(piece * 128, 128)
        inner, outer = plane_sums(nxt, 0, (2,), lanes)
        diagonal = edge_rows(outer)
        for q in range(4):
            sums[piece, 16 + q] = inner[q] + jnp.where(row_id > 0, outer[q], 0.0)
        along_y = []
        for n, plane in enumerate((0, 2, 4, 6)):
            inner, outer = plane_sums(nxt, plane, (0, 1) if plane == 0 else (0, 1, 2), lanes)
            along_y.append(edge_rows(outer))
            for q in range(4):
                sums[piece, n * 4 + q] = inner[q] + jnp.where(row_id > 0, outer[q], 0.0)
        for q in range(4):
            for n in range(4):
                at = pl.ds(n * 32 + q * 8, 8)
                field[piece, at, :] = sums[piece, n * 4 + q, pl.ds(0, 8, stride=2), :]
                if n == 0:
                    beyond[piece, at, :] = sums[piece, 16 + q, pl.ds(0, 8, stride=2), :]
                else:
                    second = (None, along_y[0][q], diagonal[q], 0.0)[n]
                    beyond[piece, at, :] = jnp.where(
                        first_row, along_y[n][q], jnp.where(second_row, second, 0.0)
                    )
        turned[0, piece * 128 : (piece + 1) * 128, :] = jnp.transpose(field[piece])
        turned[1, piece * 128 : (piece + 1) * 128, :] = jnp.transpose(beyond[piece])
    for f in range(2):
        for b in range(2):
            parcel[pl.ds(2 * f + b, NDEV, stride=4), :] = turned[f, pl.ds(2 * b, NDEV, stride=4), :]

    pl.semaphore_wait(barrier, NDEV - 1)

    def remote(src, dst, ssem, rsem, to):
        return pltpu.make_async_remote_copy(
            src_ref=src, dst_ref=dst, send_sem=ssem, recv_sem=rsem, device_id=to, device_id_type=MESH
        )

    faces = [
        remote(nxt.at[2, :, :, 0], xr_up, bulk_ssem.at[0], bulk_rsem.at[0], (gx_up, gy)),
        remote(nxt.at[0, :, :, 7], xr_dn, bulk_ssem.at[1], bulk_rsem.at[1], (gx_dn, gy)),
        remote(nxt.at[:, 2, :, :, pl.ds(0, 1)], yr_up, bulk_ssem.at[2], bulk_rsem.at[2], (gx, gy_up)),
        remote(nxt.at[:, 0, :, :, pl.ds(15, 1)], yr_dn, bulk_ssem.at[3], bulk_rsem.at[3], (gx, gy_dn)),
        remote(nxt.at[2, 2, :, 0, pl.ds(0, 1)], corner.at[0], bulk_ssem.at[4], bulk_rsem.at[4], (gx_up, gy_up)),
        remote(nxt.at[2, 0, :, 0, pl.ds(15, 1)], corner.at[1], bulk_ssem.at[5], bulk_rsem.at[5], (gx_up, gy_dn)),
        remote(nxt.at[0, 2, :, 7, pl.ds(0, 1)], corner.at[2], bulk_ssem.at[6], bulk_rsem.at[6], (gx_dn, gy_up)),
        remote(nxt.at[0, 0, :, 7, pl.ds(15, 1)], corner.at[3], bulk_ssem.at[7], bulk_rsem.at[7], (gx_dn, gy_dn)),
    ]
    def to_all(source, target, index, rows):
        place = target.at[pl.ds(me * rows, rows)]
        for peer in peers:
            remote(source(peer), place, ex_ssem.at[index], ex_rsem.at[index], peer).start()
        pltpu.make_async_copy(source((gx, gy)), place, ex_rsem.at[index]).start()

    def all_here(target, index):
        pltpu.make_async_copy(target, target, ex_rsem.at[index]).wait()

    def all_sent(target, index, rows):
        part = target.at[pl.ds(0, (NDEV - 1) * rows)]
        pltpu.make_async_copy(part, part, ex_ssem.at[index]).wait()

    to_all(lambda peer: parcel.at[pl.ds(4 * (peer[0] * 4 + peer[1]), 4)], arrived, 0, 4)

    age_copy.wait()
    decay = [
        jnp.exp(jnp.full((8, 128), age[j], jnp.int32).astype(jnp.float32) * (-1.0 / age_span))
        for j in range(SNAPS)
    ]
    recent_copy.wait()
    for j in range(1, SNAPS):
        for k in range(24):
            at = pl.ds(j * ROWS + k * 8, 8)
            snaps[at, :] = snaps[at, :] * decay[j]
    modes_copy.wait()

    def project(block, carry):
        base = block * (4 * ROWS)
        acc = [[None] * 4 for _ in range(7)]
        for k in range(24):
            u = [modes[pl.ds(pl.multiple_of(base + n * ROWS + k * 8, 8), 8), :] for n in range(4)]
            for j in range(7):
                a = snaps[pl.ds((j + 1) * ROWS + k * 8, 8), :]
                for n in range(4):
                    term = a * u[n]
                    acc[j][n] = term if acc[j][n] is None else acc[j][n] + term
        for j in range(7):
            rows = [jnp.sum(acc[j][n], axis=0, keepdims=True) for n in range(4)]
            for n in range(4):
                stack[pl.ds((j + 1) * RANK + block * 4 + n, 1), :] = rows[n]
        return carry

    lax.fori_loop(0, RANK // 4, project, 0)
    ones = jnp.ones((8, 128), jnp.float32)

    def row_totals(block):
        return lax.dot_general(
            ones, block, (((1,), (1,)), ((), ())), precision=HIGHEST, preferred_element_type=jnp.float32
        )

    stack[0:RANK, :] = jnp.zeros((RANK, 128), jnp.float32)
    for r in range(4):
        mine1[r : r + 1, :] = row_totals(stack[r * 128 : (r + 1) * 128, :])[0:1]


    to_all(lambda peer: mine1.at[pl.ds(0, 4)], got1, 1, 4)

    all_here(arrived, 0)
    lane = lax.broadcasted_iota(jnp.int32, (32, 128), 1)
    lane_block = lax.rem(lax.div(lane, 8), 4)
    in_x, in_y = lax.div(lane, 32), lax.rem(lane, 8)

    def lane_roll(value, by):
        by = by % 128
        return pltpu.roll(value, by, 1) if by else value

    def from_before(value):
        return pltpu.roll(value, 1, 0)

    def pick(values):
        out = values[0]
        for g in range(1, 4):
            out = jnp.where(lane_block == g, values[g], out)
        return out

    for b in range(2):
        own = [arrived[pl.ds(4 * g + b, 32, stride=16), :] for g in range(4)]
        other = [arrived[pl.ds(4 * g + 2 + b, 32, stride=16), :] for g in range(4)]
        whole = []
        for g in range(4):
            below = other[(g + 3) % 4]
            corners = lane_roll(below, -33) + from_before(lane_roll(below, -65))
            whole.append(
                own[g]
                + jnp.where(in_x == 0, from_before(other[g]), jnp.where(in_y == 0, below, 0.0))
                + jnp.where((in_x == 0) & (in_y == 0), corners, 0.0)
            )
        scale = vel_gain / pick([lane_roll(whole[g], g * 8) for g in range(4)])
        for c in range(3):
            moved = pick([lane_roll(whole[g], (g - c - 1) * 8) for g in range(4)])
            snaps[pl.ds(c * 64 + b, 32, stride=2), :] = moved * scale
    fresh = [snaps[k * 8 : (k + 1) * 8, :] * decay[0] for k in range(24)]
    for k in range(24):
        snaps[k * 8 : (k + 1) * 8, :] = fresh[k]

    def project_fresh(block, carry):
        base = block * (8 * ROWS)
        for n in range(8):
            acc = None
            for k in range(24):
                at = pl.ds(pl.multiple_of(base + n * ROWS + k * 8, 8), 8)
                term = snaps[k * 8 : (k + 1) * 8, :] * modes[at, :]
                acc = term if acc is None else acc + term
            stack[pl.ds(block * 8 + n, 1), :] = jnp.sum(acc, axis=0, keepdims=True)
        return carry

    lax.fori_loop(0, RANK // 8, project_fresh, 0)
    mine2[...] = jnp.zeros((8, 128), jnp.float32)
    mine2[0:1, 0:RANK] = row_totals(stack[0:RANK, :])[0:1]
    to_all(lambda peer: mine2.at[pl.ds(0, 1)], got2, 2, 1)

    for copy in faces:
        copy.start()

    all_here(got1, 1)
    total = got1[0:8, :]
    for d in range(1, NDEV // 2):
        total = total + got1[d * 8 : (d + 1) * 8, :]
    total = (total[0:4] + total[4:8]) * (1.0 / TOTAL)

    def spread_row(r, row):
        spread[r * 128 : (r + 1) * 128, :] = jnp.transpose(jnp.broadcast_to(row, (128, 128)))

    for r in range(4):
        spread_row(r, total[r : r + 1])
    for j in range(1, SNAPS):
        small[j : j + 1, 0:RANK] = total[j // 2 : j // 2 + 1, (j % 2) * RANK : (j % 2 + 1) * RANK]

    def subtract(k, carry):
        base = k * 32
        acc = [
            [snaps[pl.ds(pl.multiple_of(base + j * ROWS + n * 8, 8), 8), :] for n in range(4)]
            for j in range(1, SNAPS)
        ]

        for m in range(RANK):
            u = [modes[pl.ds(pl.multiple_of(base + m * ROWS + n * 8, 8), 8), :] for n in range(4)]
            for j in range(7):
                c = spread[(j + 1) * RANK + m : (j + 1) * RANK + m + 1, :]
                for n in range(4):
                    acc[j][n] = acc[j][n] - c * u[n]
        for j in range(7):
            for n in range(4):
                resid[pl.ds(pl.multiple_of(base + (j + 1) * ROWS + n * 8, 8), 8), :] = acc[j][n]
        return carry

    lax.fori_loop(0, ROWS // 32, subtract, 0)

    def inner_products(pairs):
        acc = {}
        for k in range(24):
            r = {}
            for pair in pairs:
                for i in pair:
                    if i not in r:
                        r[i] = resid[i * ROWS + k * 8 : i * ROWS + k * 8 + 8, :]
                term = r[pair[0]] * r[pair[1]]
                acc[pair] = acc[pair] + term if pair in acc else term
        for i, j in pairs:
            stack[i * 8 + j : i * 8 + j + 1, :] = jnp.sum(acc[i, j], axis=0, keepdims=True)

    stack[0:128, :] = jnp.zeros((128, 128), jnp.float32)
    inner_products([(i, j) for i in range(1, SNAPS) for j in range(1, i + 1)])

    all_here(got2, 2)
    row = jnp.sum(got2[...], axis=0, keepdims=True) * (1.0 / TOTAL)
    small[0:1, :] = row
    spread_row(4, row)

    def subtract_fresh(k, carry):
        base = k * 64
        acc = [snaps[pl.ds(pl.multiple_of(base + n * 8, 8), 8), :] for n in range(8)]
        for m in range(RANK):
            c = spread[4 * 128 + m : 4 * 128 + m + 1, :]
            for n in range(8):
                acc[n] = acc[n] - c * modes[pl.ds(pl.multiple_of(base + m * ROWS + n * 8, 8), 8), :]
        for n in range(8):
            resid[pl.ds(pl.multiple_of(base + n * 8, 8), 8), :] = acc[n]
        return carry

    lax.fori_loop(0, ROWS // 64, subtract_fresh, 0)
    inner_products([(i, 0) for i in range(SNAPS)])
    mine3[...] = jnp.zeros((8, 128), jnp.float32)
    mine3[0:1, :] = row_totals(stack[0:128, :])[0:1]
    to_all(lambda peer: mine3.at[pl.ds(0, 1)], got3, 3, 1)
    for copy in faces:
        copy.wait()
    fixes = [
        [
            pltpu.make_async_copy(xr_up, nxt.at[2, :, :, 0], fix_sem.at[0]),
            pltpu.make_async_copy(xr_dn, nxt.at[0, :, :, 7], fix_sem.at[1]),
        ],
        [
            pltpu.make_async_copy(yr_up, nxt.at[:, 2, :, :, pl.ds(0, 1)], fix_sem.at[2]),
            pltpu.make_async_copy(yr_dn, nxt.at[:, 0, :, :, pl.ds(15, 1)], fix_sem.at[3]),
        ],
        [
            pltpu.make_async_copy(corner.at[0], nxt.at[2, 2, :, 0, pl.ds(0, 1)], fix_sem.at[4]),
            pltpu.make_async_copy(corner.at[1], nxt.at[2, 0, :, 0, pl.ds(15, 1)], fix_sem.at[5]),
            pltpu.make_async_copy(corner.at[2], nxt.at[0, 2, :, 7, pl.ds(0, 1)], fix_sem.at[6]),
            pltpu.make_async_copy(corner.at[3], nxt.at[0, 0, :, 7, pl.ds(15, 1)], fix_sem.at[7]),
        ],
    ]
    for copy in fixes[0]:
        copy.start()

    for copy in fixes[0]:
        copy.wait()
    for copy in fixes[1]:
        copy.start()
    for copy in fixes[1]:
        copy.wait()
    for copy in fixes[2]:
        copy.start()

    for copy in fixes[2]:
        copy.wait()
    all_sent(arrived, 0, 4)
    all_sent(got1, 1, 4)
    all_sent(got2, 2, 1)
    all_here(got3, 3)
    small[8:16, :] = jnp.broadcast_to(jnp.sum(got3[...], axis=0, keepdims=True) * (1.0 / TOTAL), (8, 128))
    all_sent(got3, 3, 1)


def last_kernel(nxt, resid, small, singular, nxt_out, dirs_out, core_out, dirs, gram, wide, sem):
    bulk = [
        pltpu.make_async_copy(nxt.at[e, f], nxt_out.at[e, f], sem.at[3 * e + f])
        for e in range(3)
        for f in range(3)
    ]
    for copy in bulk:
        copy.start()
    gram[...] = jnp.transpose(jnp.broadcast_to(small[8:9, :], (128, 128)))
    low = [[None] * SNAPS for _ in range(SNAPS)]
    inv_diag = [None] * SNAPS
    for j in range(SNAPS):
        diag = gram[j * 8 + j : j * 8 + j + 1, :]
        for k in range(j):
            diag = diag - low[j][k] * low[j][k]
        low[j][j] = jnp.sqrt(diag)
        inv_diag[j] = 1.0 / low[j][j]
        for i in range(j + 1, SNAPS):
            value = gram[i * 8 + j : i * 8 + j + 1, :]
            for k in range(j):
                value = value - low[i][k] * low[j][k]
            low[i][j] = value * inv_diag[j]
    inverse = [[None] * SNAPS for _ in range(SNAPS)]
    for j in range(SNAPS):
        inverse[j][j] = inv_diag[j]
        for i in range(j + 1, SNAPS):
            value = None
            for k in range(j, i):
                term = low[i][k] * inverse[k][j]
                value = term if value is None else value + term
            inverse[i][j] = -value * inv_diag[i]
    for i in range(SNAPS):
        factors = [jnp.broadcast_to(inverse[i][j], (8, 128)) for j in range(i + 1)]
        for k in range(24):
            acc = None
            for j in range(i + 1):
                term = factors[j] * resid[j * ROWS + k * 8 : j * ROWS + k * 8 + 8, :]
                acc = term if acc is None else acc + term
            dirs[i * ROWS + k * 8 : i * ROWS + k * 8 + 8, :] = acc
    out = pltpu.make_async_copy(dirs, dirs_out, sem.at[9])
    out.start()

    row_id = lax.broadcasted_iota(jnp.int32, (RANK, 128), 0)
    lane_id = lax.broadcasted_iota(jnp.int32, (RANK, 128), 1)
    wide[...] = jnp.zeros((128, 128), jnp.float32)
    wide[127:128, 0:RANK] = singular[...]
    wide[0:RANK, :] = jnp.where(row_id == lane_id, jnp.broadcast_to(wide[127:128, :], (RANK, 128)), 0.0)
    row8 = lax.broadcasted_iota(jnp.int32, (8, 128), 0)
    lane8 = lax.broadcasted_iota(jnp.int32, (8, 128), 1)
    block = jnp.where(lane8 < RANK, small[0:8, :], 0.0)
    for i in range(SNAPS):
        for j in range(i + 1):
            block = jnp.where((row8 == i) & (lane8 == RANK + j), low[i][j], block)
    wide[RANK : RANK + 8, :] = block
    core_out[...] = jnp.transpose(wide[...])[0 : RANK + 8, 0 : RANK + 8]
    for copy in bulk:
        copy.wait()
    out.wait()


def per_device(populations, solid, basis, singular, recent, age):
    f32 = jnp.float32
    vmem, hbm, smem = pltpu.VMEM, pltpu.HBM, pltpu.SMEM
    modes = basis.reshape(RANK, 3, 2, 32, 128).transpose(0, 1, 3, 2, 4).reshape(RANK * ROWS, 128)
    earlier = recent.reshape(7, 3, 2, 32, 128).transpose(0, 1, 3, 2, 4).reshape(7 * ROWS, 128)
    dma = pltpu.SemaphoreType.DMA
    in_hbm = pl.BlockSpec(memory_space=hbm)
    in_vmem = pl.BlockSpec(memory_space=vmem)
    nxt, resid, small = pl.pallas_call(
        main_kernel,
        out_shape=(
            vmem((3, 3, 3, 8, 16, 512), f32),
            vmem((SNAPS * ROWS, 128), f32),
            vmem((16, 128), f32),
        ),
        in_specs=[in_hbm] * 5,
        out_specs=(in_vmem, in_vmem, in_vmem),
        scratch_shapes=[
            vmem((27, 8, 16, 512), f32),
            vmem((8, 16, 512), jnp.int32),
            vmem((RANK * ROWS, 128), f32),
            vmem((SNAPS * ROWS, 128), f32),
            vmem((5, 16, 512), f32),
            vmem((4, 20, 16, 128), f32),
            vmem((4, 128, 128), f32),
            vmem((4, 128, 128), f32),
            vmem((2, 512, 128), f32),
            vmem((4 * NDEV, 128), f32),
            vmem((4 * NDEV, 128), f32),
            vmem((3, 3, 16, 512), f32),
            vmem((3, 3, 16, 512), f32),
            vmem((3, 3, 8, 1, 512), f32),
            vmem((3, 3, 8, 1, 512), f32),
            vmem((4, 3, 1, 512), f32),
            vmem((SNAPS * RANK, 128), f32),
            vmem((8, 128), f32),
            vmem((NDEV * 4, 128), f32),
            vmem((8, 128), f32),
            vmem((NDEV, 128), f32),
            vmem((8, 128), f32),
            vmem((NDEV, 128), f32),
            vmem((5 * 128, 128), f32),
            smem((8,), jnp.int32),
            dma((12,)),
            dma((8,)),
            dma((8,)),
            dma((4,)),
            dma((4,)),
            dma((8,)),
        ],
        compiler_params=pltpu.CompilerParams(
            collective_id=0, has_side_effects=True, vmem_limit_bytes=40 * 2**20
        ),
    )(*(pltpu.with_memory_space_constraint(a, hbm) for a in (populations, solid, modes, earlier, age)))
    nxt_out, dirs, core = pl.pallas_call(
        last_kernel,
        out_shape=(
            jax.ShapeDtypeStruct((3, 3, 3, 8, 16, 512), f32),
            jax.ShapeDtypeStruct((SNAPS * ROWS, 128), f32),
            jax.ShapeDtypeStruct((RANK + 8, RANK + 8), f32),
        ),
        in_specs=[in_vmem, in_vmem, in_vmem, in_vmem],
        out_specs=(in_hbm, in_hbm, in_vmem),
        scratch_shapes=[vmem((SNAPS * ROWS, 128), f32), vmem((128, 128), f32), vmem((128, 128), f32), dma((10,))],
        compiler_params=pltpu.CompilerParams(vmem_limit_bytes=24 * 2**20),
    )(nxt, resid, small, singular.reshape(1, RANK))
    directions = dirs.reshape(SNAPS, 3, 32, 2, 128).transpose(0, 1, 3, 2, 4).reshape(SNAPS, 3, 2, 4096)
    return nxt_out.reshape(27, 8, 16, 512), directions, core


def solution(mesh):
    return jax.shard_map(
        per_device,
        mesh=mesh,
        in_specs=(
            P(None, "gx", "gy", None),
            P("gx", "gy", None),
            P(None, None, ("gx", "gy"), None),
            P(),
            P(None, None, ("gx", "gy"), None),
            P(),
        ),
        out_specs=(P(None, "gx", "gy", None), P(None, None, ("gx", "gy"), None), P()),
        check_vma=False,
    )
```

```python
import functools

import jax
import jax.numpy as jnp
from jax import lax
from jax.experimental import pallas as pl
from jax.experimental.pallas import tpu as pltpu
from jax.sharding import PartitionSpec as P

MESH = pl.DeviceIdType.MESH
EARLY_FACES = 6
HIGHEST = lax.Precision.HIGHEST
omega_rate = 1.0 / 0.6
keep_rate = 1.0 - omega_rate
vel_gain = 50.0
age_span = 8.0
WEIGHTS = (8.0 / 27.0, 2.0 / 27.0, 1.0 / 54.0, 1.0 / 216.0)
NDEV = 128
RANK = 64
SNAPS = 8
ROWS = 192
TOTAL = 3145728.0


def direction(i):
    return i // 9 - 1, i // 3 % 3 - 1, i % 3 - 1


def shifted(value, shift_y, shift_z):
    if shift_z:
        value = pltpu.roll(value, 1 if shift_z > 0 else value.shape[1] - 1, 1)
    if shift_y:
        value = pltpu.roll(value, 1 if shift_y > 0 else value.shape[0] - 1, 0)
    return value


def collide_plane(x, pops, solid, mo, nxt):
    for piece in range(4):
        lanes = pl.ds(piece * 128, 128)
        total = [None] * 4
        for e in range(3):
            row = [None] * 3
            for f in range(3):
                p0, p1, p2 = (pops[9 * e + 3 * f + g, x, :, lanes] for g in range(3))
                row[f] = (p0 + p1 + p2, p2 - p0)
            dens = row[0][0] + row[1][0] + row[2][0]
            my = row[2][0] - row[0][0]
            mz = row[0][1] + row[1][1] + row[2][1]
            if e == 0:
                total = [dens, -dens, my, mz]
            else:
                total = [
                    total[0] + dens,
                    total[1] + dens if e == 2 else total[1],
                    total[2] + my,
                    total[3] + mz,
                ]
        inv = 1.0 / total[0]
        ux, uy, uz = total[1] * inv, total[2] * inv, total[3] * inv
        scaled = omega_rate * total[0]
        mo[0, :, lanes] = scaled
        mo[1, :, lanes] = ux
        mo[2, :, lanes] = uy
        mo[3, :, lanes] = uz
        mo[4, :, lanes] = scaled * (1.0 - 1.5 * (ux * ux + uy * uy + uz * uz))

    x_up, x_down = lax.rem(x + 1, 8), lax.rem(x + 7, 8)
    place = {0: x, 1: x_up, -1: x_down}
    for pos in range(14, 27):
        neg = 26 - pos
        ex, ey, ez = direction(pos)
        weight = WEIGHTS[abs(ex) + abs(ey) + abs(ez)]
        along = None
        for axis, part in enumerate((ex, ey, ez)):
            if part:
                term = mo[1 + axis]
                if along is None:
                    along = term if part > 0 else -term
                else:
                    along = along + term if part > 0 else along - term
        is_solid = solid[x] > 0
        scaled = mo[0] * along
        even = weight * mo[4] + (4.5 * weight) * (scaled * along)
        odd = (3.0 * weight) * scaled
        p_pos, p_neg = pops[pos, x], pops[neg, x]
        r_pos = jnp.where(is_solid, p_neg, keep_rate * p_pos + (even + odd))
        r_neg = jnp.where(is_solid, p_pos, keep_rate * p_neg + (even - odd))
        nxt[ex + 1, ey + 1, ez + 1, place[ex]] = shifted(r_pos, ey, ez)
        nxt[1 - ex, 1 - ey, 1 - ez, place[-ex]] = shifted(r_neg, -ey, -ez)
    still = pops[13, x]
    nxt[1, 1, 1, x] = jnp.where(solid[x] > 0, still, keep_rate * still + WEIGHTS[0] * mo[4])


def plane_sums(nxt, plane, firsts, lanes):
    inner, outer = None, None
    for e in firsts:
        row = []
        for f in range(3):
            p0, p1, p2 = (nxt[e, f, g, plane, :, lanes] for g in range(3))
            row.append((p0 + p1 + p2, p2 - p0))
        dens = row[0][0] + row[1][0]
        now_in = [dens, (e - 1) * dens if e != 1 else None, -row[0][0], row[0][1] + row[1][1]]
        now_out = [row[2][0], (e - 1) * row[2][0] if e != 1 else None, row[2][0], row[2][1]]
        if inner is None:
            inner, outer = now_in, now_out
        else:
            inner = [a if b is None else b if a is None else a + b for a, b in zip(inner, now_in)]
            outer = [a if b is None else b if a is None else a + b for a, b in zip(outer, now_out)]
    return inner, outer


def main_kernel(
    pops_in, solid_in, modes_in, recent_in, age_in,
    nxt, resid, small,
    pops, solid, modes, snaps, mo, sums, field, beyond, turned, parcel, arrived, xr_up, xr_dn, yr_up, yr_dn, corner,
    stack, pair1, mine1, got1, mine2, got2, mine3, got3, spread,
    age, load_sem, pair_sem, bulk_ssem, bulk_rsem, ex_ssem, ex_rsem, fix_sem,
):
    gx, gy = lax.axis_index("gx"), lax.axis_index("gy")
    me = gx * 4 + gy
    gx_up, gx_dn = lax.rem(gx + 1, 32), lax.rem(gx + 31, 32)
    gy_up, gy_dn = lax.rem(gy + 1, 4), lax.rem(gy + 3, 4)

    z_hi, x_at, y_at = lax.div(gx, 16), lax.rem(lax.div(gx, 4), 4), lax.rem(gx, 4)
    z_lo, core_at = lax.div(gy, 2), lax.rem(gy, 2)
    z_part = [lax.rem(z_hi + 1 + j, 2) * 16 for j in range(2)]
    x_part = [lax.rem(x_at + 2 + j, 4) * 4 for j in range(4)]
    y_part = [lax.rem(y_at + 2 + j, 4) for j in range(4)]
    lo_part = [lax.rem(z_lo + j, 2) * 2 for j in range(2)]
    core_part = [lax.rem(core_at + j, 2) for j in range(2)]
    peers = []
    for jx in (0, 1, 3, 2):
        for jy in (0, 1, 3, 2):
            for jz in range(2):
                for jl in range(2):
                    for jc in range(2):
                        if (jx, jy, jz, jl, jc) != (2, 2, 1, 0, 0):
                            peers.append((z_part[jz] + x_part[jx] + y_part[jy], lo_part[jl] + core_part[jc]))

    solid_copy = pltpu.make_async_copy(solid_in, solid, load_sem.at[8])
    solid_copy.start()

    def plane_copy(x):
        return pltpu.make_async_copy(pops_in.at[:, x], pops.at[:, x], load_sem.at[x])

    for x in (7, 0, 1, 2, 3, 4, 5, 6):
        plane_copy(x).start()
    recent_copy = pltpu.make_async_copy(recent_in, snaps.at[pl.ds(ROWS, 7 * ROWS)], load_sem.at[9])
    recent_copy.start()
    modes_copy = pltpu.make_async_copy(modes_in, modes, load_sem.at[10])
    modes_copy.start()
    age_copy = pltpu.make_async_copy(age_in, age, load_sem.at[11])
    age_copy.start()

    barrier = pltpu.get_barrier_semaphore()
    for peer in peers:
        pl.semaphore_signal(barrier, inc=1, device_id=peer, device_id_type=MESH)
    solid_copy.wait()

    def collide(k, carry):
        x = lax.rem(k + 7, 8)
        plane_copy(x).wait()
        collide_plane(x, pops, solid, mo, nxt)
        return carry

    lax.fori_loop(0, 8, collide, 0)

    row_id = lax.broadcasted_iota(jnp.int32, (16, 128), 0)
    first_row = lax.broadcasted_iota(jnp.int32, (8, 128), 0) == 0
    second_row = lax.broadcasted_iota(jnp.int32, (8, 128), 0) == 1

    def edge_rows(outer):
        return [jnp.broadcast_to(value[0:1], (8, 128)) for value in outer]

    for piece in range(4):
        lanes = pl.ds(piece * 128, 128)
        inner, outer = plane_sums(nxt, 0, (2,), lanes)
        diagonal = edge_rows(outer)
        for q in range(4):
            sums[piece, 16 + q] = inner[q] + jnp.where(row_id > 0, outer[q], 0.0)
        along_y = []
        for n, plane in enumerate((0, 2, 4, 6)):
            inner, outer = plane_sums(nxt, plane, (0, 1) if plane == 0 else (0, 1, 2), lanes)
            along_y.append(edge_rows(outer))
            for q in range(4):
                sums[piece, n * 4 + q] = inner[q] + jnp.where(row_id > 0, outer[q], 0.0)
        for q in range(4):
            for n in range(4):
                at = pl.ds(n * 32 + q * 8, 8)
                field[piece, at, :] = sums[piece, n * 4 + q, pl.ds(0, 8, stride=2), :]
                if n == 0:
                    beyond[piece, at, :] = sums[piece, 16 + q, pl.ds(0, 8, stride=2), :]
                else:
                    second = (None, along_y[0][q], diagonal[q], 0.0)[n]
                    beyond[piece, at, :] = jnp.where(
                        first_row, along_y[n][q], jnp.where(second_row, second, 0.0)
                    )
        turned[0, piece * 128 : (piece + 1) * 128, :] = jnp.transpose(field[piece])
        turned[1, piece * 128 : (piece + 1) * 128, :] = jnp.transpose(beyond[piece])
    for f in range(2):
        for b in range(2):
            parcel[pl.ds(2 * f + b, NDEV, stride=4), :] = turned[f, pl.ds(2 * b, NDEV, stride=4), :]

    pl.semaphore_wait(barrier, NDEV - 1)

    def remote(src, dst, ssem, rsem, to):
        return pltpu.make_async_remote_copy(
            src_ref=src, dst_ref=dst, send_sem=ssem, recv_sem=rsem, device_id=to, device_id_type=MESH
        )

    def x_face(n, up):
        e, plane, to, held = (2, 0, gx_up, xr_up) if up else (0, 7, gx_dn, xr_dn)
        f, g = lax.div(n, 3), lax.rem(n, 3)
        at = n if up else n + 9
        return remote(nxt.at[e, f, g, plane], held.at[f, g], bulk_ssem.at[at], bulk_rsem.at[at], (to, gy))

    others = [
        remote(nxt.at[:, 2, :, :, pl.ds(0, 1)], yr_up, bulk_ssem.at[18], bulk_rsem.at[18], (gx, gy_up)),
        remote(nxt.at[:, 0, :, :, pl.ds(15, 1)], yr_dn, bulk_ssem.at[19], bulk_rsem.at[19], (gx, gy_dn)),
        remote(nxt.at[2, 2, :, 0, pl.ds(0, 1)], corner.at[0], bulk_ssem.at[20], bulk_rsem.at[20], (gx_up, gy_up)),
        remote(nxt.at[2, 0, :, 0, pl.ds(15, 1)], corner.at[1], bulk_ssem.at[21], bulk_rsem.at[21], (gx_up, gy_dn)),
        remote(nxt.at[0, 2, :, 7, pl.ds(0, 1)], corner.at[2], bulk_ssem.at[22], bulk_rsem.at[22], (gx_dn, gy_up)),
        remote(nxt.at[0, 0, :, 7, pl.ds(15, 1)], corner.at[3], bulk_ssem.at[23], bulk_rsem.at[23], (gx_dn, gy_dn)),
    ]
    def start_faces(first, last):
        for n in range(first, last):
            x_face(jnp.int32(n), True).start()
            x_face(jnp.int32(n), False).start()

    def to_all(source, target, index, rows):
        place = target.at[pl.ds(me * rows, rows)]
        for peer in peers:
            remote(source(peer), place, ex_ssem.at[index], ex_rsem.at[index], peer).start()
        pltpu.make_async_copy(source((gx, gy)), place, ex_rsem.at[index]).start()

    def all_here(target, index):
        pltpu.make_async_copy(target, target, ex_rsem.at[index]).wait()

    def all_sent(target, index, rows):
        part = target.at[pl.ds(0, (NDEV - 1) * rows)]
        pltpu.make_async_copy(part, part, ex_ssem.at[index]).wait()

    to_all(lambda peer: parcel.at[pl.ds(4 * (peer[0] * 4 + peer[1]), 4)], arrived, 0, 4)

    age_copy.wait()
    decay = [
        jnp.exp(jnp.full((8, 128), age[j], jnp.int32).astype(jnp.float32) * (-1.0 / age_span))
        for j in range(SNAPS)
    ]
    recent_copy.wait()
    for j in range(1, SNAPS):
        for k in range(24):
            at = pl.ds(j * ROWS + k * 8, 8)
            snaps[at, :] = snaps[at, :] * decay[j]
    modes_copy.wait()

    def project(block, carry):
        base = block * (4 * ROWS)
        acc = [[None] * 4 for _ in range(7)]
        for k in range(24):
            u = [modes[pl.ds(pl.multiple_of(base + n * ROWS + k * 8, 8), 8), :] for n in range(4)]
            for j in range(7):
                a = snaps[pl.ds((j + 1) * ROWS + k * 8, 8), :]
                for n in range(4):
                    term = a * u[n]
                    acc[j][n] = term if acc[j][n] is None else acc[j][n] + term
        for j in range(7):
            rows = [jnp.sum(acc[j][n], axis=0, keepdims=True) for n in range(4)]
            for n in range(4):
                stack[pl.ds((j + 1) * RANK + block * 4 + n, 1), :] = rows[n]
        return carry

    lax.fori_loop(0, RANK // 4, project, 0)
    ones = jnp.ones((8, 128), jnp.float32)

    def row_totals(block):
        return lax.dot_general(
            ones, block, (((1,), (1,)), ((), ())), precision=HIGHEST, preferred_element_type=jnp.float32
        )

    stack[0:RANK, :] = jnp.zeros((RANK, 128), jnp.float32)
    for r in range(4):
        mine1[r : r + 1, :] = row_totals(stack[r * 128 : (r + 1) * 128, :])[0:1]


    other_core = gy + 1 - 2 * core_at
    swap = remote(
        mine1.at[pl.ds(2 - 2 * core_at, 2)], pair1.at[pl.ds(0, 2)], pair_sem.at[0], pair_sem.at[1], (gx, other_core)
    )
    swap.start()
    swap.wait()
    mine1[4:6, :] = jnp.where(core_at == 0, mine1[0:2, :], mine1[2:4, :]) + pair1[0:2, :]
    to_all(lambda peer: mine1.at[pl.ds(4, 2)], got1, 1, 2)

    all_here(arrived, 0)
    lane = lax.broadcasted_iota(jnp.int32, (32, 128), 1)
    lane_block = lax.rem(lax.div(lane, 8), 4)
    in_x, in_y = lax.div(lane, 32), lax.rem(lane, 8)

    def lane_roll(value, by):
        by = by % 128
        return pltpu.roll(value, by, 1) if by else value

    def from_before(value):
        return pltpu.roll(value, 1, 0)

    def pick(values):
        out = values[0]
        for g in range(1, 4):
            out = jnp.where(lane_block == g, values[g], out)
        return out

    for b in range(2):
        own = [arrived[pl.ds(4 * g + b, 32, stride=16), :] for g in range(4)]
        other = [arrived[pl.ds(4 * g + 2 + b, 32, stride=16), :] for g in range(4)]
        whole = []
        for g in range(4):
            below = other[(g + 3) % 4]
            corners = lane_roll(below, -33) + from_before(lane_roll(below, -65))
            whole.append(
                own[g]
                + jnp.where(in_x == 0, from_before(other[g]), jnp.where(in_y == 0, below, 0.0))
                + jnp.where((in_x == 0) & (in_y == 0), corners, 0.0)
            )
        scale = vel_gain / pick([lane_roll(whole[g], g * 8) for g in range(4)])
        for c in range(3):
            moved = pick([lane_roll(whole[g], (g - c - 1) * 8) for g in range(4)])
            snaps[pl.ds(c * 64 + b, 32, stride=2), :] = moved * scale
    fresh = [snaps[k * 8 : (k + 1) * 8, :] * decay[0] for k in range(24)]
    for k in range(24):
        snaps[k * 8 : (k + 1) * 8, :] = fresh[k]

    def project_fresh(block, carry):
        base = block * (8 * ROWS)
        for n in range(8):
            acc = None
            for k in range(24):
                at = pl.ds(pl.multiple_of(base + n * ROWS + k * 8, 8), 8)
                term = fresh[k] * modes[at, :]
                acc = term if acc is None else acc + term
            stack[pl.ds(block * 8 + n, 1), :] = jnp.sum(acc, axis=0, keepdims=True)
        return carry

    lax.fori_loop(0, RANK // 8, project_fresh, 0)
    mine2[...] = jnp.zeros((8, 128), jnp.float32)
    mine2[0:1, 0:RANK] = row_totals(stack[0:RANK, :])[0:1]
    to_all(lambda peer: mine2.at[pl.ds(0, 1)], got2, 2, 1)

    start_faces(0, EARLY_FACES)
    for copy in others:
        copy.start()

    all_here(got1, 1)
    total = got1[0:8, :]
    for d in range(1, NDEV // 4):
        total = total + got1[d * 8 : (d + 1) * 8, :]
    total = (total[0:4] + total[4:8]) * (1.0 / TOTAL)

    def spread_row(r, row):
        spread[r * 128 : (r + 1) * 128, :] = jnp.transpose(jnp.broadcast_to(row, (128, 128)))

    for r in range(4):
        spread_row(r, total[r : r + 1])
    for j in range(1, SNAPS):
        small[j : j + 1, 0:RANK] = total[j // 2 : j // 2 + 1, (j % 2) * RANK : (j % 2 + 1) * RANK]

    def subtract(k, carry):
        base = k * 32
        acc = [
            [snaps[pl.ds(pl.multiple_of(base + j * ROWS + n * 8, 8), 8), :] for n in range(4)]
            for j in range(1, SNAPS)
        ]

        for m in range(RANK):
            u = [modes[pl.ds(pl.multiple_of(base + m * ROWS + n * 8, 8), 8), :] for n in range(4)]
            for j in range(7):
                c = spread[(j + 1) * RANK + m : (j + 1) * RANK + m + 1, :]
                for n in range(4):
                    acc[j][n] = acc[j][n] - c * u[n]
        for j in range(7):
            for n in range(4):
                resid[pl.ds(pl.multiple_of(base + (j + 1) * ROWS + n * 8, 8), 8), :] = acc[j][n]
        return carry

    lax.fori_loop(0, ROWS // 32, subtract, 0)

    def inner_products(pairs):
        acc = {}
        for k in range(24):
            r = {}
            for pair in pairs:
                for i in pair:
                    if i not in r:
                        r[i] = resid[i * ROWS + k * 8 : i * ROWS + k * 8 + 8, :]
                term = r[pair[0]] * r[pair[1]]
                acc[pair] = acc[pair] + term if pair in acc else term
        for i, j in pairs:
            stack[i * 8 + j : i * 8 + j + 1, :] = jnp.sum(acc[i, j], axis=0, keepdims=True)

    stack[0:128, :] = jnp.zeros((128, 128), jnp.float32)
    inner_products([(i, j) for i in range(1, SNAPS) for j in range(1, i + 1)])

    all_here(got2, 2)
    row = jnp.sum(got2[...], axis=0, keepdims=True) * (1.0 / TOTAL)
    small[0:1, :] = row
    spread_row(4, row)

    def subtract_fresh(k, carry):
        base = k * 64
        acc = [snaps[pl.ds(pl.multiple_of(base + n * 8, 8), 8), :] for n in range(8)]
        for m in range(RANK):
            c = spread[4 * 128 + m : 4 * 128 + m + 1, :]
            for n in range(8):
                acc[n] = acc[n] - c * modes[pl.ds(pl.multiple_of(base + m * ROWS + n * 8, 8), 8), :]
        for n in range(8):
            resid[pl.ds(pl.multiple_of(base + n * 8, 8), 8), :] = acc[n]
        return carry

    lax.fori_loop(0, ROWS // 64, subtract_fresh, 0)
    inner_products([(i, 0) for i in range(SNAPS)])
    mine3[...] = jnp.zeros((8, 128), jnp.float32)
    mine3[0:1, :] = row_totals(stack[0:128, :])[0:1]
    to_all(lambda peer: mine3.at[pl.ds(0, 1)], got3, 3, 1)
    start_faces(EARLY_FACES, 9)
    fixes = [
        pltpu.make_async_copy(yr_up, nxt.at[:, 2, :, :, pl.ds(0, 1)], fix_sem.at[0]),
        pltpu.make_async_copy(yr_dn, nxt.at[:, 0, :, :, pl.ds(15, 1)], fix_sem.at[1]),
        pltpu.make_async_copy(xr_up, nxt.at[2, :, :, 0], fix_sem.at[2]),
        pltpu.make_async_copy(xr_dn, nxt.at[0, :, :, 7], fix_sem.at[3]),
        pltpu.make_async_copy(corner.at[0], nxt.at[2, 2, :, 0, pl.ds(0, 1)], fix_sem.at[4]),
        pltpu.make_async_copy(corner.at[1], nxt.at[2, 0, :, 0, pl.ds(15, 1)], fix_sem.at[5]),
        pltpu.make_async_copy(corner.at[2], nxt.at[0, 2, :, 7, pl.ds(0, 1)], fix_sem.at[6]),
        pltpu.make_async_copy(corner.at[3], nxt.at[0, 0, :, 7, pl.ds(15, 1)], fix_sem.at[7]),
    ]
    for copy in others:
        copy.wait()

    def face_sent(n, carry):
        x_face(n, True).wait_send()
        x_face(n, False).wait_send()
        return carry

    def face_here(n, carry):
        x_face(n, True).wait_recv()
        x_face(n, False).wait_recv()
        return carry

    lax.fori_loop(0, EARLY_FACES, face_sent, 0)
    lax.fori_loop(0, EARLY_FACES, face_here, 0)
    lax.fori_loop(EARLY_FACES, 9, face_sent, 0)
    for copy in fixes[0:2]:
        copy.start()
    for copy in fixes[0:2]:
        copy.wait()
    lax.fori_loop(EARLY_FACES, 9, face_here, 0)
    for copy in fixes[2:4]:
        copy.start()
    for copy in fixes[2:4]:
        copy.wait()
    for copy in fixes[4:8]:
        copy.start()
    for copy in fixes[4:8]:
        copy.wait()
    all_sent(arrived, 0, 4)
    all_sent(got1, 1, 2)
    all_sent(got2, 2, 1)
    all_here(got3, 3)
    small[8:16, :] = jnp.broadcast_to(jnp.sum(got3[...], axis=0, keepdims=True) * (1.0 / TOTAL), (8, 128))
    all_sent(got3, 3, 1)


def last_kernel(nxt, resid, small, singular, nxt_out, dirs_out, core_out, dirs, gram, wide, sem):
    bulk = [
        pltpu.make_async_copy(nxt.at[e, f], nxt_out.at[e, f], sem.at[3 * e + f])
        for e in range(3)
        for f in range(3)
    ]
    for copy in bulk:
        copy.start()
    gram[...] = jnp.transpose(jnp.broadcast_to(small[8:9, :], (128, 128)))
    low = [[None] * SNAPS for _ in range(SNAPS)]
    inv_diag = [None] * SNAPS
    for j in range(SNAPS):
        diag = gram[j * 8 + j : j * 8 + j + 1, :]
        for k in range(j):
            diag = diag - low[j][k] * low[j][k]
        low[j][j] = jnp.sqrt(diag)
        inv_diag[j] = 1.0 / low[j][j]
        for i in range(j + 1, SNAPS):
            value = gram[i * 8 + j : i * 8 + j + 1, :]
            for k in range(j):
                value = value - low[i][k] * low[j][k]
            low[i][j] = value * inv_diag[j]
    inverse = [[None] * SNAPS for _ in range(SNAPS)]
    for j in range(SNAPS):
        inverse[j][j] = inv_diag[j]
        for i in range(j + 1, SNAPS):
            value = None
            for k in range(j, i):
                term = low[i][k] * inverse[k][j]
                value = term if value is None else value + term
            inverse[i][j] = -value * inv_diag[i]
    for i in range(SNAPS):
        factors = [jnp.broadcast_to(inverse[i][j], (8, 128)) for j in range(i + 1)]
        for k in range(24):
            acc = None
            for j in range(i + 1):
                term = factors[j] * resid[j * ROWS + k * 8 : j * ROWS + k * 8 + 8, :]
                acc = term if acc is None else acc + term
            dirs[i * ROWS + k * 8 : i * ROWS + k * 8 + 8, :] = acc
    out = pltpu.make_async_copy(dirs, dirs_out, sem.at[9])
    out.start()

    row_id = lax.broadcasted_iota(jnp.int32, (RANK, 128), 0)
    lane_id = lax.broadcasted_iota(jnp.int32, (RANK, 128), 1)
    wide[...] = jnp.zeros((128, 128), jnp.float32)
    wide[127:128, 0:RANK] = singular[...]
    wide[0:RANK, :] = jnp.where(row_id == lane_id, jnp.broadcast_to(wide[127:128, :], (RANK, 128)), 0.0)
    row8 = lax.broadcasted_iota(jnp.int32, (8, 128), 0)
    lane8 = lax.broadcasted_iota(jnp.int32, (8, 128), 1)
    block = jnp.where(lane8 < RANK, small[0:8, :], 0.0)
    for i in range(SNAPS):
        for j in range(i + 1):
            block = jnp.where((row8 == i) & (lane8 == RANK + j), low[i][j], block)
    wide[RANK : RANK + 8, :] = block
    core_out[...] = jnp.transpose(wide[...])[0 : RANK + 8, 0 : RANK + 8]
    for copy in bulk:
        copy.wait()
    out.wait()


def per_device(populations, solid, basis, singular, recent, age):
    f32 = jnp.float32
    vmem, hbm, smem = pltpu.VMEM, pltpu.HBM, pltpu.SMEM
    modes = basis.reshape(RANK, 3, 2, 32, 128).transpose(0, 1, 3, 2, 4).reshape(RANK * ROWS, 128)
    earlier = recent.reshape(7, 3, 2, 32, 128).transpose(0, 1, 3, 2, 4).reshape(7 * ROWS, 128)
    dma = pltpu.SemaphoreType.DMA
    in_hbm = pl.BlockSpec(memory_space=hbm)
    in_vmem = pl.BlockSpec(memory_space=vmem)
    nxt, resid, small = pl.pallas_call(
        main_kernel,
        out_shape=(
            vmem((3, 3, 3, 8, 16, 512), f32),
            vmem((SNAPS * ROWS, 128), f32),
            vmem((16, 128), f32),
        ),
        in_specs=[in_hbm] * 5,
        out_specs=(in_vmem, in_vmem, in_vmem),
        scratch_shapes=[
            vmem((27, 8, 16, 512), f32),
            vmem((8, 16, 512), jnp.int32),
            vmem((RANK * ROWS, 128), f32),
            vmem((SNAPS * ROWS, 128), f32),
            vmem((5, 16, 512), f32),
            vmem((4, 20, 16, 128), f32),
            vmem((4, 128, 128), f32),
            vmem((4, 128, 128), f32),
            vmem((2, 512, 128), f32),
            vmem((4 * NDEV, 128), f32),
            vmem((4 * NDEV, 128), f32),
            vmem((3, 3, 16, 512), f32),
            vmem((3, 3, 16, 512), f32),
            vmem((3, 3, 8, 1, 512), f32),
            vmem((3, 3, 8, 1, 512), f32),
            vmem((4, 3, 1, 512), f32),
            vmem((SNAPS * RANK, 128), f32),
            vmem((8, 128), f32),
            vmem((8, 128), f32),
            vmem((NDEV * 2, 128), f32),
            vmem((8, 128), f32),
            vmem((NDEV, 128), f32),
            vmem((8, 128), f32),
            vmem((NDEV, 128), f32),
            vmem((5 * 128, 128), f32),
            smem((8,), jnp.int32),
            dma((12,)),
            dma((2,)),
            dma((24,)),
            dma((24,)),
            dma((4,)),
            dma((4,)),
            dma((8,)),
        ],
        compiler_params=pltpu.CompilerParams(
            collective_id=0, has_side_effects=True, vmem_limit_bytes=40 * 2**20
        ),
    )(*(pltpu.with_memory_space_constraint(a, hbm) for a in (populations, solid, modes, earlier, age)))
    nxt_out, dirs, core = pl.pallas_call(
        last_kernel,
        out_shape=(
            jax.ShapeDtypeStruct((3, 3, 3, 8, 16, 512), f32),
            jax.ShapeDtypeStruct((SNAPS * ROWS, 128), f32),
            jax.ShapeDtypeStruct((RANK + 8, RANK + 8), f32),
        ),
        in_specs=[in_vmem, in_vmem, in_vmem, in_vmem],
        out_specs=(in_hbm, in_hbm, in_vmem),
        scratch_shapes=[vmem((SNAPS * ROWS, 128), f32), vmem((128, 128), f32), vmem((128, 128), f32), dma((10,))],
        compiler_params=pltpu.CompilerParams(vmem_limit_bytes=24 * 2**20),
    )(nxt, resid, small, singular.reshape(1, RANK))
    directions = dirs.reshape(SNAPS, 3, 32, 2, 128).transpose(0, 1, 3, 2, 4).reshape(SNAPS, 3, 2, 4096)
    return nxt_out.reshape(27, 8, 16, 512), directions, core


def solution(mesh):
    return jax.shard_map(
        per_device,
        mesh=mesh,
        in_specs=(
            P(None, "gx", "gy", None),
            P("gx", "gy", None),
            P(None, None, ("gx", "gy"), None),
            P(),
            P(None, None, ("gx", "gy"), None),
            P(),
        ),
        out_specs=(P(None, "gx", "gy", None), P(None, None, ("gx", "gy"), None), P()),
        check_vma=False,
    )
```

```python
import functools

import jax
import jax.numpy as jnp
from jax import lax
from jax.experimental import pallas as pl
from jax.experimental.pallas import tpu as pltpu
from jax.sharding import PartitionSpec as P

MESH = pl.DeviceIdType.MESH
EARLY_FACES = 6
omega_rate = 1.0 / 0.6
keep_rate = 1.0 - omega_rate
vel_gain = 50.0
age_span = 8.0
WEIGHTS = (8.0 / 27.0, 2.0 / 27.0, 1.0 / 54.0, 1.0 / 216.0)
NDEV = 128
RANK = 64
SNAPS = 8
ROWS = 192
TOTAL = 3145728.0


def direction(i):
    return i // 9 - 1, i // 3 % 3 - 1, i % 3 - 1


def shifted(value, shift_y, shift_z):
    if shift_z:
        value = pltpu.roll(value, 1 if shift_z > 0 else value.shape[1] - 1, 1)
    if shift_y:
        value = pltpu.roll(value, 1 if shift_y > 0 else value.shape[0] - 1, 0)
    return value


def collide_plane(x, pops, solid, mo, nxt):
    for piece in range(4):
        lanes = pl.ds(piece * 128, 128)
        total = [None] * 4
        for e in range(3):
            row = [None] * 3
            for f in range(3):
                p0, p1, p2 = (pops[9 * e + 3 * f + g, x, :, lanes] for g in range(3))
                row[f] = (p0 + p1 + p2, p2 - p0)
            dens = row[0][0] + row[1][0] + row[2][0]
            my = row[2][0] - row[0][0]
            mz = row[0][1] + row[1][1] + row[2][1]
            if e == 0:
                total = [dens, -dens, my, mz]
            else:
                total = [
                    total[0] + dens,
                    total[1] + dens if e == 2 else total[1],
                    total[2] + my,
                    total[3] + mz,
                ]
        inv = 1.0 / total[0]
        ux, uy, uz = total[1] * inv, total[2] * inv, total[3] * inv
        scaled = omega_rate * total[0]
        mo[0, :, lanes] = scaled
        mo[1, :, lanes] = ux
        mo[2, :, lanes] = uy
        mo[3, :, lanes] = uz
        mo[4, :, lanes] = scaled * (1.0 - 1.5 * (ux * ux + uy * uy + uz * uz))

    x_up, x_down = lax.rem(x + 1, 8), lax.rem(x + 7, 8)
    place = {0: x, 1: x_up, -1: x_down}
    for pos in range(14, 27):
        neg = 26 - pos
        ex, ey, ez = direction(pos)
        weight = WEIGHTS[abs(ex) + abs(ey) + abs(ez)]
        along = None
        for axis, part in enumerate((ex, ey, ez)):
            if part:
                term = mo[1 + axis]
                if along is None:
                    along = term if part > 0 else -term
                else:
                    along = along + term if part > 0 else along - term
        is_solid = solid[x] > 0
        scaled = mo[0] * along
        even = weight * mo[4] + (4.5 * weight) * (scaled * along)
        odd = (3.0 * weight) * scaled
        p_pos, p_neg = pops[pos, x], pops[neg, x]
        r_pos = jnp.where(is_solid, p_neg, keep_rate * p_pos + (even + odd))
        r_neg = jnp.where(is_solid, p_pos, keep_rate * p_neg + (even - odd))
        nxt[ex + 1, ey + 1, ez + 1, place[ex]] = shifted(r_pos, ey, ez)
        nxt[1 - ex, 1 - ey, 1 - ez, place[-ex]] = shifted(r_neg, -ey, -ez)
    still = pops[13, x]
    nxt[1, 1, 1, x] = jnp.where(solid[x] > 0, still, keep_rate * still + WEIGHTS[0] * mo[4])


def plane_sums(nxt, plane, firsts, lanes):
    inner, outer = None, None
    for e in firsts:
        row = []
        for f in range(3):
            p0, p1, p2 = (nxt[e, f, g, plane, :, lanes] for g in range(3))
            row.append((p0 + p1 + p2, p2 - p0))
        dens = row[0][0] + row[1][0]
        now_in = [dens, (e - 1) * dens if e != 1 else None, -row[0][0], row[0][1] + row[1][1]]
        now_out = [row[2][0], (e - 1) * row[2][0] if e != 1 else None, row[2][0], row[2][1]]
        if inner is None:
            inner, outer = now_in, now_out
        else:
            inner = [a if b is None else b if a is None else a + b for a, b in zip(inner, now_in)]
            outer = [a if b is None else b if a is None else a + b for a, b in zip(outer, now_out)]
    return inner, outer


def main_kernel(
    pops_in, solid_in, modes_in, recent_in, age_in,
    nxt, resid, small,
    pops, solid, modes, snaps, mo, sums, field, beyond, turned, parcel, arrived, xr_up, xr_dn, yr_up, yr_dn, corner,
    stack, pair1, mine1, got1, mine2, got2, mine3, got3, spread,
    age, load_sem, pair_sem, bulk_ssem, bulk_rsem, ex_ssem, ex_rsem, fix_sem,
):
    gx, gy = lax.axis_index("gx"), lax.axis_index("gy")
    me = gx * 4 + gy
    gx_up, gx_dn = lax.rem(gx + 1, 32), lax.rem(gx + 31, 32)
    gy_up, gy_dn = lax.rem(gy + 1, 4), lax.rem(gy + 3, 4)

    z_hi, x_at, y_at = lax.div(gx, 16), lax.rem(lax.div(gx, 4), 4), lax.rem(gx, 4)
    z_lo, core_at = lax.div(gy, 2), lax.rem(gy, 2)
    z_part = [lax.rem(z_hi + 1 + j, 2) * 16 for j in range(2)]
    x_part = [lax.rem(x_at + 2 + j, 4) * 4 for j in range(4)]
    y_part = [lax.rem(y_at + 2 + j, 4) for j in range(4)]
    lo_part = [lax.rem(z_lo + j, 2) * 2 for j in range(2)]
    core_part = [lax.rem(core_at + j, 2) for j in range(2)]
    peers = []
    for jx in (0, 1, 3, 2):
        for jy in (0, 1, 3, 2):
            for jz in range(2):
                for jl in range(2):
                    for jc in range(2):
                        if (jx, jy, jz, jl, jc) != (2, 2, 1, 0, 0):
                            peers.append((z_part[jz] + x_part[jx] + y_part[jy], lo_part[jl] + core_part[jc]))

    solid_copy = pltpu.make_async_copy(solid_in, solid, load_sem.at[8])
    solid_copy.start()

    def plane_copy(x):
        return pltpu.make_async_copy(pops_in.at[:, x], pops.at[:, x], load_sem.at[x])

    for x in (7, 0, 1, 2, 3, 4, 5, 6):
        plane_copy(x).start()
    recent_copy = pltpu.make_async_copy(recent_in, snaps.at[pl.ds(ROWS, 7 * ROWS)], load_sem.at[9])
    recent_copy.start()
    modes_copy = pltpu.make_async_copy(modes_in, modes, load_sem.at[10])
    modes_copy.start()
    age_copy = pltpu.make_async_copy(age_in, age, load_sem.at[11])
    age_copy.start()

    barrier = pltpu.get_barrier_semaphore()
    for peer in peers:
        pl.semaphore_signal(barrier, inc=1, device_id=peer, device_id_type=MESH)
    solid_copy.wait()

    def collide(k, carry):
        x = lax.rem(k + 7, 8)
        plane_copy(x).wait()
        collide_plane(x, pops, solid, mo, nxt)
        return carry

    lax.fori_loop(0, 8, collide, 0)

    row_id = lax.broadcasted_iota(jnp.int32, (16, 128), 0)
    first_row = lax.broadcasted_iota(jnp.int32, (8, 128), 0) == 0
    second_row = lax.broadcasted_iota(jnp.int32, (8, 128), 0) == 1

    def edge_rows(outer):
        return [jnp.broadcast_to(value[0:1], (8, 128)) for value in outer]

    for piece in range(4):
        lanes = pl.ds(piece * 128, 128)
        inner, outer = plane_sums(nxt, 0, (2,), lanes)
        diagonal = edge_rows(outer)
        for q in range(4):
            sums[piece, 16 + q] = inner[q] + jnp.where(row_id > 0, outer[q], 0.0)
        along_y = []
        for n, plane in enumerate((0, 2, 4, 6)):
            inner, outer = plane_sums(nxt, plane, (0, 1) if plane == 0 else (0, 1, 2), lanes)
            along_y.append(edge_rows(outer))
            for q in range(4):
                sums[piece, n * 4 + q] = inner[q] + jnp.where(row_id > 0, outer[q], 0.0)
        for q in range(4):
            for n in range(4):
                at = pl.ds(n * 32 + q * 8, 8)
                field[piece, at, :] = sums[piece, n * 4 + q, pl.ds(0, 8, stride=2), :]
                if n == 0:
                    beyond[piece, at, :] = sums[piece, 16 + q, pl.ds(0, 8, stride=2), :]
                else:
                    second = (None, along_y[0][q], diagonal[q], 0.0)[n]
                    beyond[piece, at, :] = jnp.where(
                        first_row, along_y[n][q], jnp.where(second_row, second, 0.0)
                    )
        turned[0, piece * 128 : (piece + 1) * 128, :] = jnp.transpose(field[piece])
        turned[1, piece * 128 : (piece + 1) * 128, :] = jnp.transpose(beyond[piece])
    for f in range(2):
        for b in range(2):
            parcel[pl.ds(2 * f + b, NDEV, stride=4), :] = turned[f, pl.ds(2 * b, NDEV, stride=4), :]

    pl.semaphore_wait(barrier, NDEV - 1)

    def remote(src, dst, ssem, rsem, to):
        return pltpu.make_async_remote_copy(
            src_ref=src, dst_ref=dst, send_sem=ssem, recv_sem=rsem, device_id=to, device_id_type=MESH
        )

    def x_face(n, up):
        e, plane, to, held = (2, 0, gx_up, xr_up) if up else (0, 7, gx_dn, xr_dn)
        f, g = lax.div(n, 3), lax.rem(n, 3)
        at = n if up else n + 9
        return remote(nxt.at[e, f, g, plane], held.at[f, g], bulk_ssem.at[at], bulk_rsem.at[at], (to, gy))

    others = [
        remote(nxt.at[:, 2, :, :, pl.ds(0, 1)], yr_up, bulk_ssem.at[18], bulk_rsem.at[18], (gx, gy_up)),
        remote(nxt.at[:, 0, :, :, pl.ds(15, 1)], yr_dn, bulk_ssem.at[19], bulk_rsem.at[19], (gx, gy_dn)),
        remote(nxt.at[2, 2, :, 0, pl.ds(0, 1)], corner.at[0], bulk_ssem.at[20], bulk_rsem.at[20], (gx_up, gy_up)),
        remote(nxt.at[2, 0, :, 0, pl.ds(15, 1)], corner.at[1], bulk_ssem.at[21], bulk_rsem.at[21], (gx_up, gy_dn)),
        remote(nxt.at[0, 2, :, 7, pl.ds(0, 1)], corner.at[2], bulk_ssem.at[22], bulk_rsem.at[22], (gx_dn, gy_up)),
        remote(nxt.at[0, 0, :, 7, pl.ds(15, 1)], corner.at[3], bulk_ssem.at[23], bulk_rsem.at[23], (gx_dn, gy_dn)),
    ]
    def start_faces(first, last):
        for n in range(first, last):
            x_face(jnp.int32(n), True).start()
            x_face(jnp.int32(n), False).start()

    def to_all(source, target, index, rows):
        place = target.at[pl.ds(me * rows, rows)]
        for peer in peers:
            remote(source(peer), place, ex_ssem.at[index], ex_rsem.at[index], peer).start()
        pltpu.make_async_copy(source((gx, gy)), place, ex_rsem.at[index]).start()

    def all_here(target, index):
        pltpu.make_async_copy(target, target, ex_rsem.at[index]).wait()

    def all_sent(target, index, rows):
        part = target.at[pl.ds(0, (NDEV - 1) * rows)]
        pltpu.make_async_copy(part, part, ex_ssem.at[index]).wait()

    to_all(lambda peer: parcel.at[pl.ds(4 * (peer[0] * 4 + peer[1]), 4)], arrived, 0, 4)

    age_copy.wait()
    decay = [
        jnp.exp(jnp.full((8, 128), age[j], jnp.int32).astype(jnp.float32) * (-1.0 / age_span))
        for j in range(SNAPS)
    ]
    recent_copy.wait()
    for j in range(1, SNAPS):
        for k in range(24):
            at = pl.ds(j * ROWS + k * 8, 8)
            snaps[at, :] = snaps[at, :] * decay[j]
    modes_copy.wait()

    def project(block, carry):
        base = block * (4 * ROWS)
        acc = [[None] * 4 for _ in range(7)]
        for k in range(24):
            u = [modes[pl.ds(pl.multiple_of(base + n * ROWS + k * 8, 8), 8), :] for n in range(4)]
            for j in range(7):
                a = snaps[pl.ds((j + 1) * ROWS + k * 8, 8), :]
                for n in range(4):
                    term = a * u[n]
                    acc[j][n] = term if acc[j][n] is None else acc[j][n] + term
        for j in range(7):
            rows = [jnp.sum(acc[j][n], axis=0, keepdims=True) for n in range(4)]
            for n in range(4):
                stack[pl.ds((j + 1) * RANK + block * 4 + n, 1), :] = rows[n]
        return carry

    lax.fori_loop(0, RANK // 4, project, 0)

    def row_totals(block):
        return jnp.sum(jnp.transpose(block), axis=0, keepdims=True)

    stack[0:RANK, :] = jnp.zeros((RANK, 128), jnp.float32)
    for r in range(4):
        mine1[r : r + 1, :] = row_totals(stack[r * 128 : (r + 1) * 128, :])


    other_core = gy + 1 - 2 * core_at
    swap = remote(
        mine1.at[pl.ds(2 - 2 * core_at, 2)], pair1.at[pl.ds(0, 2)], pair_sem.at[0], pair_sem.at[1], (gx, other_core)
    )
    swap.start()
    swap.wait()
    mine1[4:6, :] = jnp.where(core_at == 0, mine1[0:2, :], mine1[2:4, :]) + pair1[0:2, :]
    to_all(lambda peer: mine1.at[pl.ds(4, 2)], got1, 1, 2)

    all_here(arrived, 0)
    lane = lax.broadcasted_iota(jnp.int32, (32, 128), 1)
    lane_block = lax.rem(lax.div(lane, 8), 4)
    in_x, in_y = lax.div(lane, 32), lax.rem(lane, 8)

    def lane_roll(value, by):
        by = by % 128
        return pltpu.roll(value, by, 1) if by else value

    def from_before(value):
        return pltpu.roll(value, 1, 0)

    def pick(values):
        out = values[0]
        for g in range(1, 4):
            out = jnp.where(lane_block == g, values[g], out)
        return out

    for b in range(2):
        own = [arrived[pl.ds(4 * g + b, 32, stride=16), :] for g in range(4)]
        other = [arrived[pl.ds(4 * g + 2 + b, 32, stride=16), :] for g in range(4)]
        whole = []
        for g in range(4):
            below = other[(g + 3) % 4]
            corners = lane_roll(below, -33) + from_before(lane_roll(below, -65))
            whole.append(
                own[g]
                + jnp.where(in_x == 0, from_before(other[g]), jnp.where(in_y == 0, below, 0.0))
                + jnp.where((in_x == 0) & (in_y == 0), corners, 0.0)
            )
        scale = vel_gain / pick([lane_roll(whole[g], g * 8) for g in range(4)])
        for c in range(3):
            moved = pick([lane_roll(whole[g], (g - c - 1) * 8) for g in range(4)])
            snaps[pl.ds(c * 64 + b, 32, stride=2), :] = moved * scale
    fresh = [snaps[k * 8 : (k + 1) * 8, :] * decay[0] for k in range(24)]
    for k in range(24):
        snaps[k * 8 : (k + 1) * 8, :] = fresh[k]

    def project_fresh(block, carry):
        base = block * (8 * ROWS)
        for n in range(8):
            acc = None
            for k in range(24):
                at = pl.ds(pl.multiple_of(base + n * ROWS + k * 8, 8), 8)
                term = fresh[k] * modes[at, :]
                acc = term if acc is None else acc + term
            stack[pl.ds(block * 8 + n, 1), :] = jnp.sum(acc, axis=0, keepdims=True)
        return carry

    lax.fori_loop(0, RANK // 8, project_fresh, 0)
    mine2[...] = jnp.zeros((8, 128), jnp.float32)
    mine2[0:1, :] = row_totals(stack[0:128, :])
    to_all(lambda peer: mine2.at[pl.ds(0, 1)], got2, 2, 1)

    start_faces(0, EARLY_FACES)
    for copy in others:
        copy.start()

    all_here(got1, 1)
    total = got1[0:8, :]
    for d in range(1, NDEV // 4):
        total = total + got1[d * 8 : (d + 1) * 8, :]
    total = (total[0:4] + total[4:8]) * (1.0 / TOTAL)

    def spread_row(r, row):
        spread[r * 128 : (r + 1) * 128, :] = jnp.transpose(jnp.broadcast_to(row, (128, 128)))

    for r in range(4):
        spread_row(r, total[r : r + 1])
    for j in range(1, SNAPS):
        small[j : j + 1, 0:RANK] = total[j // 2 : j // 2 + 1, (j % 2) * RANK : (j % 2 + 1) * RANK]

    def subtract(k, carry):
        base = k * 32
        acc = [
            [snaps[pl.ds(pl.multiple_of(base + j * ROWS + n * 8, 8), 8), :] for n in range(4)]
            for j in range(1, SNAPS)
        ]

        for m in range(RANK):
            u = [modes[pl.ds(pl.multiple_of(base + m * ROWS + n * 8, 8), 8), :] for n in range(4)]
            for j in range(7):
                c = spread[(j + 1) * RANK + m : (j + 1) * RANK + m + 1, :]
                for n in range(4):
                    acc[j][n] = acc[j][n] - c * u[n]
        for j in range(7):
            for n in range(4):
                resid[pl.ds(pl.multiple_of(base + (j + 1) * ROWS + n * 8, 8), 8), :] = acc[j][n]
        return carry

    lax.fori_loop(0, ROWS // 32, subtract, 0)

    def inner_products(pairs):
        acc = {}
        for k in range(24):
            r = {}
            for pair in pairs:
                for i in pair:
                    if i not in r:
                        r[i] = resid[i * ROWS + k * 8 : i * ROWS + k * 8 + 8, :]
                term = r[pair[0]] * r[pair[1]]
                acc[pair] = acc[pair] + term if pair in acc else term
        for i, j in pairs:
            stack[i * 8 + j : i * 8 + j + 1, :] = jnp.sum(acc[i, j], axis=0, keepdims=True)

    stack[0:128, :] = jnp.zeros((128, 128), jnp.float32)
    inner_products([(i, j) for i in range(1, SNAPS) for j in range(1, i + 1)])

    all_here(got2, 2)
    row = jnp.sum(got2[...], axis=0, keepdims=True) * (1.0 / TOTAL)
    small[0:1, :] = row
    spread_row(4, row)

    def subtract_fresh(k, carry):
        base = k * 64
        acc = [snaps[pl.ds(pl.multiple_of(base + n * 8, 8), 8), :] for n in range(8)]
        for m in range(RANK):
            c = spread[4 * 128 + m : 4 * 128 + m + 1, :]
            for n in range(8):
                acc[n] = acc[n] - c * modes[pl.ds(pl.multiple_of(base + m * ROWS + n * 8, 8), 8), :]
        for n in range(8):
            resid[pl.ds(pl.multiple_of(base + n * 8, 8), 8), :] = acc[n]
        return carry

    lax.fori_loop(0, ROWS // 64, subtract_fresh, 0)
    inner_products([(i, 0) for i in range(SNAPS)])
    mine3[...] = jnp.zeros((8, 128), jnp.float32)
    mine3[0:1, :] = row_totals(stack[0:128, :])
    to_all(lambda peer: mine3.at[pl.ds(0, 1)], got3, 3, 1)
    start_faces(EARLY_FACES, 9)
    fixes = [
        pltpu.make_async_copy(yr_up, nxt.at[:, 2, :, :, pl.ds(0, 1)], fix_sem.at[0]),
        pltpu.make_async_copy(yr_dn, nxt.at[:, 0, :, :, pl.ds(15, 1)], fix_sem.at[1]),
        pltpu.make_async_copy(xr_up, nxt.at[2, :, :, 0], fix_sem.at[2]),
        pltpu.make_async_copy(xr_dn, nxt.at[0, :, :, 7], fix_sem.at[3]),
        pltpu.make_async_copy(corner.at[0], nxt.at[2, 2, :, 0, pl.ds(0, 1)], fix_sem.at[4]),
        pltpu.make_async_copy(corner.at[1], nxt.at[2, 0, :, 0, pl.ds(15, 1)], fix_sem.at[5]),
        pltpu.make_async_copy(corner.at[2], nxt.at[0, 2, :, 7, pl.ds(0, 1)], fix_sem.at[6]),
        pltpu.make_async_copy(corner.at[3], nxt.at[0, 0, :, 7, pl.ds(15, 1)], fix_sem.at[7]),
    ]
    for copy in others:
        copy.wait()

    def face_sent(n, carry):
        x_face(n, True).wait_send()
        x_face(n, False).wait_send()
        return carry

    def face_here(n, carry):
        x_face(n, True).wait_recv()
        x_face(n, False).wait_recv()
        return carry

    lax.fori_loop(0, EARLY_FACES, face_sent, 0)
    lax.fori_loop(0, EARLY_FACES, face_here, 0)
    lax.fori_loop(EARLY_FACES, 9, face_sent, 0)
    for copy in fixes[0:2]:
        copy.start()
    for copy in fixes[0:2]:
        copy.wait()
    lax.fori_loop(EARLY_FACES, 9, face_here, 0)
    for copy in fixes[2:4]:
        copy.start()
    for copy in fixes[2:4]:
        copy.wait()
    for copy in fixes[4:8]:
        copy.start()
    for copy in fixes[4:8]:
        copy.wait()
    all_sent(arrived, 0, 4)
    all_sent(got1, 1, 2)
    all_sent(got2, 2, 1)
    all_here(got3, 3)
    small[8:16, :] = jnp.broadcast_to(jnp.sum(got3[...], axis=0, keepdims=True) * (1.0 / TOTAL), (8, 128))
    all_sent(got3, 3, 1)


def last_kernel(nxt, resid, small, singular, nxt_out, dirs_out, core_out, dirs, gram, wide, sem):
    bulk = [
        pltpu.make_async_copy(nxt.at[e, f], nxt_out.at[e, f], sem.at[3 * e + f])
        for e in range(3)
        for f in range(3)
    ]
    for copy in bulk:
        copy.start()
    gram[...] = jnp.transpose(jnp.broadcast_to(small[8:9, :], (128, 128)))
    low = [[None] * SNAPS for _ in range(SNAPS)]
    inv_diag = [None] * SNAPS
    for j in range(SNAPS):
        diag = gram[j * 8 + j : j * 8 + j + 1, :]
        for k in range(j):
            diag = diag - low[j][k] * low[j][k]
        low[j][j] = jnp.sqrt(diag)
        inv_diag[j] = 1.0 / low[j][j]
        for i in range(j + 1, SNAPS):
            value = gram[i * 8 + j : i * 8 + j + 1, :]
            for k in range(j):
                value = value - low[i][k] * low[j][k]
            low[i][j] = value * inv_diag[j]
    inverse = [[None] * SNAPS for _ in range(SNAPS)]
    for j in range(SNAPS):
        inverse[j][j] = inv_diag[j]
        for i in range(j + 1, SNAPS):
            value = None
            for k in range(j, i):
                term = low[i][k] * inverse[k][j]
                value = term if value is None else value + term
            inverse[i][j] = -value * inv_diag[i]
    for i in range(SNAPS):
        factors = [jnp.broadcast_to(inverse[i][j], (8, 128)) for j in range(i + 1)]
        for k in range(24):
            acc = None
            for j in range(i + 1):
                term = factors[j] * resid[j * ROWS + k * 8 : j * ROWS + k * 8 + 8, :]
                acc = term if acc is None else acc + term
            dirs[i * ROWS + k * 8 : i * ROWS + k * 8 + 8, :] = acc
    out = pltpu.make_async_copy(dirs, dirs_out, sem.at[9])
    out.start()

    row_id = lax.broadcasted_iota(jnp.int32, (RANK, 128), 0)
    lane_id = lax.broadcasted_iota(jnp.int32, (RANK, 128), 1)
    wide[...] = jnp.zeros((128, 128), jnp.float32)
    wide[127:128, 0:RANK] = singular[...]
    wide[0:RANK, :] = jnp.where(row_id == lane_id, jnp.broadcast_to(wide[127:128, :], (RANK, 128)), 0.0)
    row8 = lax.broadcasted_iota(jnp.int32, (8, 128), 0)
    lane8 = lax.broadcasted_iota(jnp.int32, (8, 128), 1)
    block = jnp.where(lane8 < RANK, small[0:8, :], 0.0)
    for i in range(SNAPS):
        for j in range(i + 1):
            block = jnp.where((row8 == i) & (lane8 == RANK + j), low[i][j], block)
    wide[RANK : RANK + 8, :] = block
    core_out[...] = jnp.transpose(wide[...])[0 : RANK + 8, 0 : RANK + 8]
    for copy in bulk:
        copy.wait()
    out.wait()


def per_device(populations, solid, basis, singular, recent, age):
    f32 = jnp.float32
    vmem, hbm, smem = pltpu.VMEM, pltpu.HBM, pltpu.SMEM
    modes = basis.reshape(RANK, 3, 2, 32, 128).transpose(0, 1, 3, 2, 4).reshape(RANK * ROWS, 128)
    earlier = recent.reshape(7, 3, 2, 32, 128).transpose(0, 1, 3, 2, 4).reshape(7 * ROWS, 128)
    dma = pltpu.SemaphoreType.DMA
    in_hbm = pl.BlockSpec(memory_space=hbm)
    in_vmem = pl.BlockSpec(memory_space=vmem)
    nxt, resid, small = pl.pallas_call(
        main_kernel,
        out_shape=(
            vmem((3, 3, 3, 8, 16, 512), f32),
            vmem((SNAPS * ROWS, 128), f32),
            vmem((16, 128), f32),
        ),
        in_specs=[in_hbm] * 5,
        out_specs=(in_vmem, in_vmem, in_vmem),
        scratch_shapes=[
            vmem((27, 8, 16, 512), f32),
            vmem((8, 16, 512), jnp.int32),
            vmem((RANK * ROWS, 128), f32),
            vmem((SNAPS * ROWS, 128), f32),
            vmem((5, 16, 512), f32),
            vmem((4, 20, 16, 128), f32),
            vmem((4, 128, 128), f32),
            vmem((4, 128, 128), f32),
            vmem((2, 512, 128), f32),
            vmem((4 * NDEV, 128), f32),
            vmem((4 * NDEV, 128), f32),
            vmem((3, 3, 16, 512), f32),
            vmem((3, 3, 16, 512), f32),
            vmem((3, 3, 8, 1, 512), f32),
            vmem((3, 3, 8, 1, 512), f32),
            vmem((4, 3, 1, 512), f32),
            vmem((SNAPS * RANK, 128), f32),
            vmem((8, 128), f32),
            vmem((8, 128), f32),
            vmem((NDEV * 2, 128), f32),
            vmem((8, 128), f32),
            vmem((NDEV, 128), f32),
            vmem((8, 128), f32),
            vmem((NDEV, 128), f32),
            vmem((5 * 128, 128), f32),
            smem((8,), jnp.int32),
            dma((12,)),
            dma((2,)),
            dma((24,)),
            dma((24,)),
            dma((4,)),
            dma((4,)),
            dma((8,)),
        ],
        compiler_params=pltpu.CompilerParams(
            collective_id=0, has_side_effects=True, vmem_limit_bytes=40 * 2**20
        ),
    )(*(pltpu.with_memory_space_constraint(a, hbm) for a in (populations, solid, modes, earlier, age)))
    nxt_out, dirs, core = pl.pallas_call(
        last_kernel,
        out_shape=(
            jax.ShapeDtypeStruct((3, 3, 3, 8, 16, 512), f32),
            jax.ShapeDtypeStruct((SNAPS * ROWS, 128), f32),
            jax.ShapeDtypeStruct((RANK + 8, RANK + 8), f32),
        ),
        in_specs=[in_vmem, in_vmem, in_vmem, in_vmem],
        out_specs=(in_hbm, in_hbm, in_vmem),
        scratch_shapes=[vmem((SNAPS * ROWS, 128), f32), vmem((128, 128), f32), vmem((128, 128), f32), dma((10,))],
        compiler_params=pltpu.CompilerParams(vmem_limit_bytes=24 * 2**20),
    )(nxt, resid, small, singular.reshape(1, RANK))
    directions = dirs.reshape(SNAPS, 3, 32, 2, 128).transpose(0, 1, 3, 2, 4).reshape(SNAPS, 3, 2, 4096)
    return nxt_out.reshape(27, 8, 16, 512), directions, core


def solution(mesh):
    return jax.shard_map(
        per_device,
        mesh=mesh,
        in_specs=(
            P(None, "gx", "gy", None),
            P("gx", "gy", None),
            P(None, None, ("gx", "gy"), None),
            P(),
            P(None, None, ("gx", "gy"), None),
            P(),
        ),
        out_specs=(P(None, "gx", "gy", None), P(None, None, ("gx", "gy"), None), P()),
        check_vma=False,
    )
```

```python
import functools

import jax
import jax.numpy as jnp
from jax import lax
from jax.experimental import pallas as pl
from jax.experimental.pallas import tpu as pltpu
from jax.sharding import PartitionSpec as P

MESH = pl.DeviceIdType.MESH
EARLY_FACES = 6
omega_rate = 1.0 / 0.6
keep_rate = 1.0 - omega_rate
vel_gain = 50.0
age_span = 8.0
WEIGHTS = (8.0 / 27.0, 2.0 / 27.0, 1.0 / 54.0, 1.0 / 216.0)
NDEV = 128
RANK = 64
SNAPS = 8
ROWS = 192
TOTAL = 3145728.0


def direction(i):
    return i // 9 - 1, i // 3 % 3 - 1, i % 3 - 1


def shifted(value, shift_y, shift_z):
    if shift_z:
        value = pltpu.roll(value, 1 if shift_z > 0 else value.shape[1] - 1, 1)
    if shift_y:
        value = pltpu.roll(value, 1 if shift_y > 0 else value.shape[0] - 1, 0)
    return value


def collide_plane(x, pops, solid, mo, nxt):
    for piece in range(4):
        lanes = pl.ds(piece * 128, 128)
        total = [None] * 4
        for e in range(3):
            row = [None] * 3
            for f in range(3):
                p0, p1, p2 = (pops[9 * e + 3 * f + g, x, :, lanes] for g in range(3))
                row[f] = (p0 + p1 + p2, p2 - p0)
            dens = row[0][0] + row[1][0] + row[2][0]
            my = row[2][0] - row[0][0]
            mz = row[0][1] + row[1][1] + row[2][1]
            if e == 0:
                total = [dens, -dens, my, mz]
            else:
                total = [
                    total[0] + dens,
                    total[1] + dens if e == 2 else total[1],
                    total[2] + my,
                    total[3] + mz,
                ]
        inv = 1.0 / total[0]
        ux, uy, uz = total[1] * inv, total[2] * inv, total[3] * inv
        scaled = omega_rate * total[0]
        mo[0, :, lanes] = scaled
        mo[1, :, lanes] = ux
        mo[2, :, lanes] = uy
        mo[3, :, lanes] = uz
        mo[4, :, lanes] = scaled * (1.0 - 1.5 * (ux * ux + uy * uy + uz * uz))

    x_up, x_down = lax.rem(x + 1, 8), lax.rem(x + 7, 8)
    place = {0: x, 1: x_up, -1: x_down}
    for pos in range(14, 27):
        neg = 26 - pos
        ex, ey, ez = direction(pos)
        weight = WEIGHTS[abs(ex) + abs(ey) + abs(ez)]
        along = None
        for axis, part in enumerate((ex, ey, ez)):
            if part:
                term = mo[1 + axis]
                if along is None:
                    along = term if part > 0 else -term
                else:
                    along = along + term if part > 0 else along - term
        is_solid = solid[x] > 0
        scaled = mo[0] * along
        even = weight * mo[4] + (4.5 * weight) * (scaled * along)
        odd = (3.0 * weight) * scaled
        p_pos, p_neg = pops[pos, x], pops[neg, x]
        r_pos = jnp.where(is_solid, p_neg, keep_rate * p_pos + (even + odd))
        r_neg = jnp.where(is_solid, p_pos, keep_rate * p_neg + (even - odd))
        nxt[ex + 1, ey + 1, ez + 1, place[ex]] = shifted(r_pos, ey, ez)
        nxt[1 - ex, 1 - ey, 1 - ez, place[-ex]] = shifted(r_neg, -ey, -ez)
    still = pops[13, x]
    nxt[1, 1, 1, x] = jnp.where(solid[x] > 0, still, keep_rate * still + WEIGHTS[0] * mo[4])


def plane_sums(nxt, plane, firsts, lanes):
    inner, outer = None, None
    for e in firsts:
        row = []
        for f in range(3):
            p0, p1, p2 = (nxt[e, f, g, plane, :, lanes] for g in range(3))
            row.append((p0 + p1 + p2, p2 - p0))
        dens = row[0][0] + row[1][0]
        now_in = [dens, (e - 1) * dens if e != 1 else None, -row[0][0], row[0][1] + row[1][1]]
        now_out = [row[2][0], (e - 1) * row[2][0] if e != 1 else None, row[2][0], row[2][1]]
        if inner is None:
            inner, outer = now_in, now_out
        else:
            inner = [a if b is None else b if a is None else a + b for a, b in zip(inner, now_in)]
            outer = [a if b is None else b if a is None else a + b for a, b in zip(outer, now_out)]
    return inner, outer


def main_kernel(
    pops_in, solid_in, modes_in, recent_in, age_in,
    nxt, resid, small,
    pops, solid, modes, snaps, mo, sums, field, beyond, turned, parcel, arrived, xr_up, xr_dn, yr_up, yr_dn, corner,
    stack, pair1, mine1, got1, mine2, got2, mine3, got3, spread,
    age, load_sem, pair_sem, bulk_ssem, bulk_rsem, ex_ssem, ex_rsem, fix_sem,
):
    gx, gy = lax.axis_index("gx"), lax.axis_index("gy")
    me = gx * 4 + gy
    gx_up, gx_dn = lax.rem(gx + 1, 32), lax.rem(gx + 31, 32)
    gy_up, gy_dn = lax.rem(gy + 1, 4), lax.rem(gy + 3, 4)

    z_hi, x_at, y_at = lax.div(gx, 16), lax.rem(lax.div(gx, 4), 4), lax.rem(gx, 4)
    z_lo, core_at = lax.div(gy, 2), lax.rem(gy, 2)
    z_part = [lax.rem(z_hi + 1 + j, 2) * 16 for j in range(2)]
    x_part = [lax.rem(x_at + 2 + j, 4) * 4 for j in range(4)]
    y_part = [lax.rem(y_at + 2 + j, 4) for j in range(4)]
    lo_part = [lax.rem(z_lo + j, 2) * 2 for j in range(2)]
    core_part = [lax.rem(core_at + j, 2) for j in range(2)]
    peers = []
    for jx in (0, 1, 3, 2):
        for jy in (0, 1, 3, 2):
            for jz in range(2):
                for jl in range(2):
                    for jc in range(2):
                        if (jx, jy, jz, jl, jc) != (2, 2, 1, 0, 0):
                            peers.append((z_part[jz] + x_part[jx] + y_part[jy], lo_part[jl] + core_part[jc]))

    solid_copy = pltpu.make_async_copy(solid_in, solid, load_sem.at[8])
    solid_copy.start()

    def plane_copy(x):
        return pltpu.make_async_copy(pops_in.at[:, x], pops.at[:, x], load_sem.at[x])

    for x in (7, 0, 1, 2, 3, 4, 5, 6):
        plane_copy(x).start()
    recent_copy = pltpu.make_async_copy(recent_in, snaps.at[pl.ds(ROWS, 7 * ROWS)], load_sem.at[9])
    recent_copy.start()
    modes_copy = pltpu.make_async_copy(modes_in, modes, load_sem.at[10])
    modes_copy.start()
    age_copy = pltpu.make_async_copy(age_in, age, load_sem.at[11])
    age_copy.start()

    barrier = pltpu.get_barrier_semaphore()
    for peer in peers:
        pl.semaphore_signal(barrier, inc=1, device_id=peer, device_id_type=MESH)
    solid_copy.wait()

    def collide(k, carry):
        x = lax.rem(k + 7, 8)
        plane_copy(x).wait()
        collide_plane(x, pops, solid, mo, nxt)
        return carry

    lax.fori_loop(0, 8, collide, 0)

    row_id = lax.broadcasted_iota(jnp.int32, (16, 128), 0)
    first_row = lax.broadcasted_iota(jnp.int32, (8, 128), 0) == 0
    second_row = lax.broadcasted_iota(jnp.int32, (8, 128), 0) == 1

    def edge_rows(outer):
        return [jnp.broadcast_to(value[0:1], (8, 128)) for value in outer]

    for piece in range(4):
        lanes = pl.ds(piece * 128, 128)
        inner, outer = plane_sums(nxt, 0, (2,), lanes)
        diagonal = edge_rows(outer)
        for q in range(4):
            sums[piece, 16 + q] = inner[q] + jnp.where(row_id > 0, outer[q], 0.0)
        along_y = []
        for n, plane in enumerate((0, 2, 4, 6)):
            inner, outer = plane_sums(nxt, plane, (0, 1) if plane == 0 else (0, 1, 2), lanes)
            along_y.append(edge_rows(outer))
            for q in range(4):
                sums[piece, n * 4 + q] = inner[q] + jnp.where(row_id > 0, outer[q], 0.0)
        for q in range(4):
            for n in range(4):
                at = pl.ds(n * 32 + q * 8, 8)
                field[piece, at, :] = sums[piece, n * 4 + q, pl.ds(0, 8, stride=2), :]
                if n == 0:
                    beyond[piece, at, :] = sums[piece, 16 + q, pl.ds(0, 8, stride=2), :]
                else:
                    second = (None, along_y[0][q], diagonal[q], 0.0)[n]
                    beyond[piece, at, :] = jnp.where(
                        first_row, along_y[n][q], jnp.where(second_row, second, 0.0)
                    )
        turned[0, piece * 128 : (piece + 1) * 128, :] = jnp.transpose(field[piece])
        turned[1, piece * 128 : (piece + 1) * 128, :] = jnp.transpose(beyond[piece])
    for f in range(2):
        for b in range(2):
            parcel[pl.ds(2 * f + b, NDEV, stride=4), :] = turned[f, pl.ds(2 * b, NDEV, stride=4), :]

    pl.semaphore_wait(barrier, NDEV - 1)

    def remote(src, dst, ssem, rsem, to):
        return pltpu.make_async_remote_copy(
            src_ref=src, dst_ref=dst, send_sem=ssem, recv_sem=rsem, device_id=to, device_id_type=MESH
        )

    def x_face(n, up):
        e, plane, to, held = (2, 0, gx_up, xr_up) if up else (0, 7, gx_dn, xr_dn)
        f, g = lax.div(n, 3), lax.rem(n, 3)
        at = n if up else n + 9
        return remote(nxt.at[e, f, g, plane], held.at[f, g], bulk_ssem.at[at], bulk_rsem.at[at], (to, gy))

    others = [
        remote(nxt.at[:, 2, :, :, pl.ds(0, 1)], yr_up, bulk_ssem.at[18], bulk_rsem.at[18], (gx, gy_up)),
        remote(nxt.at[:, 0, :, :, pl.ds(15, 1)], yr_dn, bulk_ssem.at[19], bulk_rsem.at[19], (gx, gy_dn)),
        remote(nxt.at[2, 2, :, 0, pl.ds(0, 1)], corner.at[0], bulk_ssem.at[20], bulk_rsem.at[20], (gx_up, gy_up)),
        remote(nxt.at[2, 0, :, 0, pl.ds(15, 1)], corner.at[1], bulk_ssem.at[21], bulk_rsem.at[21], (gx_up, gy_dn)),
        remote(nxt.at[0, 2, :, 7, pl.ds(0, 1)], corner.at[2], bulk_ssem.at[22], bulk_rsem.at[22], (gx_dn, gy_up)),
        remote(nxt.at[0, 0, :, 7, pl.ds(15, 1)], corner.at[3], bulk_ssem.at[23], bulk_rsem.at[23], (gx_dn, gy_dn)),
    ]
    def start_faces(first, last):
        for n in range(first, last):
            x_face(jnp.int32(n), True).start()
            x_face(jnp.int32(n), False).start()

    def to_all(source, target, index, rows):
        place = target.at[pl.ds(me * rows, rows)]
        for peer in peers:
            remote(source(peer), place, ex_ssem.at[index], ex_rsem.at[index], peer).start()
        pltpu.make_async_copy(source((gx, gy)), place, ex_rsem.at[index]).start()

    def all_here(target, index):
        pltpu.make_async_copy(target, target, ex_rsem.at[index]).wait()

    def all_sent(target, index, rows):
        part = target.at[pl.ds(0, (NDEV - 1) * rows)]
        pltpu.make_async_copy(part, part, ex_ssem.at[index]).wait()

    to_all(lambda peer: parcel.at[pl.ds(4 * (peer[0] * 4 + peer[1]), 4)], arrived, 0, 4)

    age_copy.wait()
    decay = [
        jnp.exp(jnp.full((8, 128), age[j], jnp.int32).astype(jnp.float32) * (-1.0 / age_span))
        for j in range(SNAPS)
    ]
    recent_copy.wait()
    for j in range(1, SNAPS):
        for k in range(24):
            at = pl.ds(j * ROWS + k * 8, 8)
            snaps[at, :] = snaps[at, :] * decay[j]
    modes_copy.wait()

    def project(block, carry):
        base = block * (4 * ROWS)
        acc = [[None] * 4 for _ in range(7)]
        for k in range(24):
            u = [modes[pl.ds(pl.multiple_of(base + n * ROWS + k * 8, 8), 8), :] for n in range(4)]
            for j in range(7):
                a = snaps[pl.ds((j + 1) * ROWS + k * 8, 8), :]
                for n in range(4):
                    term = a * u[n]
                    acc[j][n] = term if acc[j][n] is None else acc[j][n] + term
        for j in range(7):
            rows = [jnp.sum(acc[j][n], axis=0, keepdims=True) for n in range(4)]
            for n in range(4):
                stack[pl.ds((j + 1) * RANK + block * 4 + n, 1), :] = rows[n]
        return carry

    lax.fori_loop(0, RANK // 4, project, 0)

    def row_totals(block):
        return jnp.sum(jnp.transpose(block), axis=0, keepdims=True)

    stack[0:RANK, :] = jnp.zeros((RANK, 128), jnp.float32)
    for r in range(4):
        mine1[r : r + 1, :] = row_totals(stack[r * 128 : (r + 1) * 128, :])


    other_core = gy + 1 - 2 * core_at
    swap = remote(
        mine1.at[pl.ds(2 - 2 * core_at, 2)], pair1.at[pl.ds(0, 2)], pair_sem.at[0], pair_sem.at[1], (gx, other_core)
    )
    swap.start()
    swap.wait()
    mine1[4:6, :] = jnp.where(core_at == 0, mine1[0:2, :], mine1[2:4, :]) + pair1[0:2, :]
    to_all(lambda peer: mine1.at[pl.ds(4, 2)], got1, 1, 2)

    all_here(arrived, 0)
    lane = lax.broadcasted_iota(jnp.int32, (32, 128), 1)
    lane_block = lax.rem(lax.div(lane, 8), 4)
    in_x, in_y = lax.div(lane, 32), lax.rem(lane, 8)

    def lane_roll(value, by):
        by = by % 128
        return pltpu.roll(value, by, 1) if by else value

    def from_before(value):
        return pltpu.roll(value, 1, 0)

    def pick(values):
        out = values[0]
        for g in range(1, 4):
            out = jnp.where(lane_block == g, values[g], out)
        return out

    for b in range(2):
        own = [arrived[pl.ds(4 * g + b, 32, stride=16), :] for g in range(4)]
        other = [arrived[pl.ds(4 * g + 2 + b, 32, stride=16), :] for g in range(4)]
        whole = []
        for g in range(4):
            below = other[(g + 3) % 4]
            corners = lane_roll(below, -33) + from_before(lane_roll(below, -65))
            whole.append(
                own[g]
                + jnp.where(in_x == 0, from_before(other[g]), jnp.where(in_y == 0, below, 0.0))
                + jnp.where((in_x == 0) & (in_y == 0), corners, 0.0)
            )
        scale = vel_gain / pick([lane_roll(whole[g], g * 8) for g in range(4)])
        for c in range(3):
            moved = pick([lane_roll(whole[g], (g - c - 1) * 8) for g in range(4)])
            snaps[pl.ds(c * 64 + b, 32, stride=2), :] = moved * scale
    fresh = [snaps[k * 8 : (k + 1) * 8, :] * decay[0] for k in range(24)]
    for k in range(24):
        snaps[k * 8 : (k + 1) * 8, :] = fresh[k]

    def project_fresh(block, carry):
        base = block * (8 * ROWS)
        for n in range(8):
            acc = None
            for k in range(24):
                at = pl.ds(pl.multiple_of(base + n * ROWS + k * 8, 8), 8)
                term = fresh[k] * modes[at, :]
                acc = term if acc is None else acc + term
            stack[pl.ds(block * 8 + n, 1), :] = jnp.sum(acc, axis=0, keepdims=True)
        return carry

    lax.fori_loop(0, RANK // 8, project_fresh, 0)
    mine2[...] = jnp.zeros((8, 128), jnp.float32)
    mine2[0:1, :] = row_totals(stack[0:128, :])
    to_all(lambda peer: mine2.at[pl.ds(0, 1)], got2, 2, 1)

    start_faces(0, EARLY_FACES)
    for copy in others:
        copy.start()

    all_here(got1, 1)
    total = got1[0:8, :]
    for d in range(1, NDEV // 4):
        total = total + got1[d * 8 : (d + 1) * 8, :]
    total = (total[0:4] + total[4:8]) * (1.0 / TOTAL)

    def spread_row(r, row):
        spread[r * 128 : (r + 1) * 128, :] = jnp.transpose(jnp.broadcast_to(row, (128, 128)))

    for r in range(4):
        spread_row(r, total[r : r + 1])
    for j in range(1, SNAPS):
        small[j : j + 1, 0:RANK] = total[j // 2 : j // 2 + 1, (j % 2) * RANK : (j % 2 + 1) * RANK]

    def subtract(k, carry):
        base = k * 32
        acc = [
            [snaps[pl.ds(pl.multiple_of(base + j * ROWS + n * 8, 8), 8), :] for n in range(4)]
            for j in range(1, SNAPS)
        ]

        for m in range(RANK):
            u = [modes[pl.ds(pl.multiple_of(base + m * ROWS + n * 8, 8), 8), :] for n in range(4)]
            for j in range(7):
                c = spread[(j + 1) * RANK + m : (j + 1) * RANK + m + 1, :]
                for n in range(4):
                    acc[j][n] = acc[j][n] - c * u[n]
        for j in range(7):
            for n in range(4):
                resid[pl.ds(pl.multiple_of(base + (j + 1) * ROWS + n * 8, 8), 8), :] = acc[j][n]
        return carry

    lax.fori_loop(0, ROWS // 32, subtract, 0)

    def inner_products(pairs):
        acc = {}
        for k in range(24):
            r = {}
            for pair in pairs:
                for i in pair:
                    if i not in r:
                        r[i] = resid[i * ROWS + k * 8 : i * ROWS + k * 8 + 8, :]
                term = r[pair[0]] * r[pair[1]]
                acc[pair] = acc[pair] + term if pair in acc else term
        for i, j in pairs:
            stack[i * 8 + j : i * 8 + j + 1, :] = jnp.sum(acc[i, j], axis=0, keepdims=True)

    stack[0:128, :] = jnp.zeros((128, 128), jnp.float32)
    inner_products([(i, j) for i in range(1, SNAPS) for j in range(1, i + 1)])

    all_here(got2, 2)
    row = jnp.sum(got2[...], axis=0, keepdims=True) * (1.0 / TOTAL)
    small[0:1, :] = row
    spread_row(4, row)

    def subtract_fresh(k, carry):
        base = k * 64
        acc = [snaps[pl.ds(pl.multiple_of(base + n * 8, 8), 8), :] for n in range(8)]
        for m in range(RANK):
            c = spread[4 * 128 + m : 4 * 128 + m + 1, :]
            for n in range(8):
                acc[n] = acc[n] - c * modes[pl.ds(pl.multiple_of(base + m * ROWS + n * 8, 8), 8), :]
        for n in range(8):
            resid[pl.ds(pl.multiple_of(base + n * 8, 8), 8), :] = acc[n]
        out = []
        for i in range(SNAPS):
            product = carry[i]
            for n in range(8):
                at = pl.ds(pl.multiple_of(base + i * ROWS + n * 8, 8), 8)
                product = product + acc[n] * (resid[at, :] if i else acc[n])
            out.append(product)
        return tuple(out)

    zero = jnp.zeros((8, 128), jnp.float32)
    products = lax.fori_loop(0, ROWS // 64, subtract_fresh, (zero,) * SNAPS)
    for i in range(SNAPS):
        stack[i * 8 : i * 8 + 1, :] = jnp.sum(products[i], axis=0, keepdims=True)
    mine3[...] = jnp.zeros((8, 128), jnp.float32)
    mine3[0:1, :] = row_totals(stack[0:128, :])
    to_all(lambda peer: mine3.at[pl.ds(0, 1)], got3, 3, 1)
    start_faces(EARLY_FACES, 9)
    fixes = [
        pltpu.make_async_copy(yr_up, nxt.at[:, 2, :, :, pl.ds(0, 1)], fix_sem.at[0]),
        pltpu.make_async_copy(yr_dn, nxt.at[:, 0, :, :, pl.ds(15, 1)], fix_sem.at[1]),
        pltpu.make_async_copy(xr_up, nxt.at[2, :, :, 0], fix_sem.at[2]),
        pltpu.make_async_copy(xr_dn, nxt.at[0, :, :, 7], fix_sem.at[3]),
        pltpu.make_async_copy(corner.at[0], nxt.at[2, 2, :, 0, pl.ds(0, 1)], fix_sem.at[4]),
        pltpu.make_async_copy(corner.at[1], nxt.at[2, 0, :, 0, pl.ds(15, 1)], fix_sem.at[5]),
        pltpu.make_async_copy(corner.at[2], nxt.at[0, 2, :, 7, pl.ds(0, 1)], fix_sem.at[6]),
        pltpu.make_async_copy(corner.at[3], nxt.at[0, 0, :, 7, pl.ds(15, 1)], fix_sem.at[7]),
    ]
    for copy in others:
        copy.wait()

    def face_sent(n, carry):
        x_face(n, True).wait_send()
        x_face(n, False).wait_send()
        return carry

    def face_here(n, carry):
        x_face(n, True).wait_recv()
        x_face(n, False).wait_recv()
        return carry

    lax.fori_loop(0, EARLY_FACES, face_sent, 0)
    lax.fori_loop(0, EARLY_FACES, face_here, 0)
    lax.fori_loop(EARLY_FACES, 9, face_sent, 0)
    for copy in fixes[0:2]:
        copy.start()
    for copy in fixes[0:2]:
        copy.wait()
    lax.fori_loop(EARLY_FACES, 9, face_here, 0)
    for copy in fixes[2:4]:
        copy.start()
    for copy in fixes[2:4]:
        copy.wait()
    for copy in fixes[4:8]:
        copy.start()
    for copy in fixes[4:8]:
        copy.wait()
    all_sent(arrived, 0, 4)
    all_sent(got1, 1, 2)
    all_sent(got2, 2, 1)
    all_here(got3, 3)
    small[8:16, :] = jnp.broadcast_to(jnp.sum(got3[...], axis=0, keepdims=True) * (1.0 / TOTAL), (8, 128))
    all_sent(got3, 3, 1)


def last_kernel(nxt, resid, small, singular, nxt_out, dirs_out, core_out, dirs, gram, wide, sem):
    bulk = [
        pltpu.make_async_copy(nxt.at[e, f], nxt_out.at[e, f], sem.at[3 * e + f])
        for e in range(3)
        for f in range(3)
    ]
    for copy in bulk:
        copy.start()
    gram[...] = jnp.transpose(jnp.broadcast_to(small[8:9, :], (128, 128)))
    low = [[None] * SNAPS for _ in range(SNAPS)]
    inv_diag = [None] * SNAPS
    for j in range(SNAPS):
        diag = gram[j * 8 + j : j * 8 + j + 1, :]
        for k in range(j):
            diag = diag - low[j][k] * low[j][k]
        low[j][j] = jnp.sqrt(diag)
        inv_diag[j] = 1.0 / low[j][j]
        for i in range(j + 1, SNAPS):
            value = gram[i * 8 + j : i * 8 + j + 1, :]
            for k in range(j):
                value = value - low[i][k] * low[j][k]
            low[i][j] = value * inv_diag[j]
    inverse = [[None] * SNAPS for _ in range(SNAPS)]
    for j in range(SNAPS):
        inverse[j][j] = inv_diag[j]
        for i in range(j + 1, SNAPS):
            value = None
            for k in range(j, i):
                term = low[i][k] * inverse[k][j]
                value = term if value is None else value + term
            inverse[i][j] = -value * inv_diag[i]
    for i in range(SNAPS):
        factors = [jnp.broadcast_to(inverse[i][j], (8, 128)) for j in range(i + 1)]
        for k in range(24):
            acc = None
            for j in range(i + 1):
                term = factors[j] * resid[j * ROWS + k * 8 : j * ROWS + k * 8 + 8, :]
                acc = term if acc is None else acc + term
            dirs[i * ROWS + k * 8 : i * ROWS + k * 8 + 8, :] = acc
    out = pltpu.make_async_copy(dirs, dirs_out, sem.at[9])
    out.start()

    row_id = lax.broadcasted_iota(jnp.int32, (RANK, 128), 0)
    lane_id = lax.broadcasted_iota(jnp.int32, (RANK, 128), 1)
    wide[...] = jnp.zeros((128, 128), jnp.float32)
    wide[127:128, 0:RANK] = singular[...]
    wide[0:RANK, :] = jnp.where(row_id == lane_id, jnp.broadcast_to(wide[127:128, :], (RANK, 128)), 0.0)
    row8 = lax.broadcasted_iota(jnp.int32, (8, 128), 0)
    lane8 = lax.broadcasted_iota(jnp.int32, (8, 128), 1)
    block = jnp.where(lane8 < RANK, small[0:8, :], 0.0)
    for i in range(SNAPS):
        for j in range(i + 1):
            block = jnp.where((row8 == i) & (lane8 == RANK + j), low[i][j], block)
    wide[RANK : RANK + 8, :] = block
    core_out[...] = jnp.transpose(wide[...])[0 : RANK + 8, 0 : RANK + 8]
    for copy in bulk:
        copy.wait()
    out.wait()


def per_device(populations, solid, basis, singular, recent, age):
    f32 = jnp.float32
    vmem, hbm, smem = pltpu.VMEM, pltpu.HBM, pltpu.SMEM
    modes = basis.reshape(RANK, 3, 2, 32, 128).transpose(0, 1, 3, 2, 4).reshape(RANK * ROWS, 128)
    earlier = recent.reshape(7, 3, 2, 32, 128).transpose(0, 1, 3, 2, 4).reshape(7 * ROWS, 128)
    dma = pltpu.SemaphoreType.DMA
    in_hbm = pl.BlockSpec(memory_space=hbm)
    in_vmem = pl.BlockSpec(memory_space=vmem)
    nxt, resid, small = pl.pallas_call(
        main_kernel,
        out_shape=(
            vmem((3, 3, 3, 8, 16, 512), f32),
            vmem((SNAPS * ROWS, 128), f32),
            vmem((16, 128), f32),
        ),
        in_specs=[in_hbm] * 5,
        out_specs=(in_vmem, in_vmem, in_vmem),
        scratch_shapes=[
            vmem((27, 8, 16, 512), f32),
            vmem((8, 16, 512), jnp.int32),
            vmem((RANK * ROWS, 128), f32),
            vmem((SNAPS * ROWS, 128), f32),
            vmem((5, 16, 512), f32),
            vmem((4, 20, 16, 128), f32),
            vmem((4, 128, 128), f32),
            vmem((4, 128, 128), f32),
            vmem((2, 512, 128), f32),
            vmem((4 * NDEV, 128), f32),
            vmem((4 * NDEV, 128), f32),
            vmem((3, 3, 16, 512), f32),
            vmem((3, 3, 16, 512), f32),
            vmem((3, 3, 8, 1, 512), f32),
            vmem((3, 3, 8, 1, 512), f32),
            vmem((4, 3, 1, 512), f32),
            vmem((SNAPS * RANK, 128), f32),
            vmem((8, 128), f32),
            vmem((8, 128), f32),
            vmem((NDEV * 2, 128), f32),
            vmem((8, 128), f32),
            vmem((NDEV, 128), f32),
            vmem((8, 128), f32),
            vmem((NDEV, 128), f32),
            vmem((5 * 128, 128), f32),
            smem((8,), jnp.int32),
            dma((12,)),
            dma((2,)),
            dma((24,)),
            dma((24,)),
            dma((4,)),
            dma((4,)),
            dma((8,)),
        ],
        compiler_params=pltpu.CompilerParams(
            collective_id=0, has_side_effects=True, vmem_limit_bytes=40 * 2**20
        ),
    )(*(pltpu.with_memory_space_constraint(a, hbm) for a in (populations, solid, modes, earlier, age)))
    nxt_out, dirs, core = pl.pallas_call(
        last_kernel,
        out_shape=(
            jax.ShapeDtypeStruct((3, 3, 3, 8, 16, 512), f32),
            jax.ShapeDtypeStruct((SNAPS * ROWS, 128), f32),
            jax.ShapeDtypeStruct((RANK + 8, RANK + 8), f32),
        ),
        in_specs=[in_vmem, in_vmem, in_vmem, in_vmem],
        out_specs=(in_hbm, in_hbm, in_vmem),
        scratch_shapes=[vmem((SNAPS * ROWS, 128), f32), vmem((128, 128), f32), vmem((128, 128), f32), dma((10,))],
        compiler_params=pltpu.CompilerParams(vmem_limit_bytes=24 * 2**20),
    )(nxt, resid, small, singular.reshape(1, RANK))
    directions = dirs.reshape(SNAPS, 3, 32, 2, 128).transpose(0, 1, 3, 2, 4).reshape(SNAPS, 3, 2, 4096)
    return nxt_out.reshape(27, 8, 16, 512), directions, core


def solution(mesh):
    return jax.shard_map(
        per_device,
        mesh=mesh,
        in_specs=(
            P(None, "gx", "gy", None),
            P("gx", "gy", None),
            P(None, None, ("gx", "gy"), None),
            P(),
            P(None, None, ("gx", "gy"), None),
            P(),
        ),
        out_specs=(P(None, "gx", "gy", None), P(None, None, ("gx", "gy"), None), P()),
        check_vma=False,
    )
```
